128 devices in a mesh: gx: 4 (over y), gy: 4 (over z), gz: 8 (over x, core).
Axes of the slice: x: 4, y: 4, z: 4, core: 2. Of those that a mesh axis runs over, the one named last changes fastest.
Arguments:
- points: float32 [262144, 512], P(('gx', 'gy', 'gz')), may hold values from -6 to 6
- order: int32 [262144], P(('gx', 'gy', 'gz')), may hold values from 0 to 262143, as said below
- near: bfloat16 [256, 1024, 1024], P(('gx', 'gy', 'gz')), may hold values from -0.1875 to 0.1875
- basis_in: bfloat16 [256, 1024, 256], P(('gx', 'gy', 'gz')), may hold values from -0.1875 to 0.1875
- basis_out: bfloat16 [256, 1024, 256], P(('gx', 'gy', 'gz')), may hold values from -0.375 to 0.375
- leaf_coupling: bfloat16 [256, 3, 256, 256], P(('gx', 'gy', 'gz')), may hold values from -0.375 to 0.375
- transfer_up: bfloat16 [128, 3, 1024, 256], P(('gx', 'gy', 'gz')), may hold values from -0.09375 to 0.09375, as said below
- transfer_down: bfloat16 [128, 3, 1024, 256], P(('gx', 'gy', 'gz')), may hold values from -0.1875 to 0.1875, as said below
- node_coupling: bfloat16 [128, 3, 3, 256, 256], P(('gx', 'gy', 'gz')), may hold values from -0.1875 to 0.1875, as said below
- ridge: float32 [1], replicated, may hold values from 0.5 to 2
Outputs:
- result: float32 [262144, 512], P(('gx', 'gy', 'gz'))
The draws below stay inside these ranges and needn't reach their ends.
Inputs may be any that keep to these rules, and one draw needn't show every extreme that they name: `order`: each device's 2048 consecutive entries are a permutation of the initial indices of those same rows. `transfer_up`: rows d and e are equal at level k whenever devices d and e have the same ancestor at level k. `transfer_down`: rows d and e are equal at level k whenever devices d and e have the same ancestor at level k. `node_coupling`: rows d and e are equal at level k whenever devices d and e have the same ancestor at level k.
All inputs are finite; a program needn't handle non-finite values.
Results may differ from the reference program's by a relative error of at most 0.014.
Values may be sent and summed in bfloat16 or wider, within the bound.
A program may use at most 128 MiB of HBM per device.

```python
import math
import jax
import jax.numpy as jnp
import numpy as np
from jax import lax

LEAF = 1024
RANK = 256
COLS = 512
LEAF_DEV = 2
LEAVES = 256
ROWS_DEV = 2048
POINTS = 262144
LEVELS = 4


def path_tables(key, tail, fan):
    device_count = LEAVES // LEAF_DEV
    devices_all = jnp.arange(device_count)
    stacked = []
    for height in range(1, LEVELS):
        nodes = LEAVES // 4 ** height
        level_key = jax.random.fold_in(key, height)
        table = jnp.clip(jax.random.normal(level_key, (nodes,) + tail, jnp.float32), -3.0, 3.0)
        stacked.append(table[LEAF_DEV * devices_all // 4 ** height] / math.sqrt(fan))
    return jnp.stack(stacked, axis=1)


def draw_transfer_up(key, part):
    return path_tables(jax.random.fold_in(key, 11), (4 * RANK, RANK), 4 * RANK).astype(jnp.bfloat16)


def draw_transfer_down(key, part):
    return path_tables(jax.random.fold_in(key, 23), (4 * RANK, RANK), RANK).astype(jnp.bfloat16)


def draw_node_coupling(key, part):
    return path_tables(jax.random.fold_in(key, 37), (3, RANK, RANK), RANK).astype(jnp.bfloat16)


def permute_block(block_key):
    return jax.random.permutation(block_key, ROWS_DEV)


def draw_order(key, part):
    device_count = POINTS // ROWS_DEV
    block_keys = jax.random.split(key, device_count)
    blocks = jax.vmap(permute_block)(block_keys)
    offsets = jnp.arange(device_count, dtype=jnp.int32)[:, None] * ROWS_DEV
    return (blocks.astype(jnp.int32) + offsets).reshape(POINTS).astype(jnp.int32)


def level_of(rng, shape, shards, least, largest):
    factor_of = 1.0
    for dim, blocks in shards:
        steps = jax.random.uniform(jax.random.fold_in(jax.random.fold_in(rng, 6), dim), (blocks,), jnp.float32, least / len(shards), largest / len(shards))
        factor_of = factor_of * jnp.repeat(jnp.exp(steps), shape[dim] // blocks).reshape((-1,) + (1,) * (len(shape) - 1 - dim))
    return factor_of


def noise(key, extent, width, most, shards=(), kind=jnp.bfloat16):
    loudness = level_of(key, extent, shards, -0.22, 0.18) if shards else 1.0
    values = jax.random.normal(key, extent, jnp.float32) * width * loudness
    return jnp.minimum(jnp.maximum(values, -most), most).astype(kind)


def setup_inputs(seed: int = 0) -> dict:
    seeds = jax.random.split(jax.random.key(seed), 11)
    points = noise(seeds[0], (POINTS, COLS), 1.0, 6.0, ((0, 128),), jnp.float32)
    order = draw_order(jax.random.fold_in(seeds[10], 71), 0)
    near = noise(seeds[2], (LEAVES, LEAF, LEAF), LEAF ** -0.5, 0.1875, ((0, 128),))
    basis_in = noise(seeds[3], (LEAVES, LEAF, RANK), LEAF ** -0.5, 0.1875, ((0, 128),))
    basis_out = noise(seeds[4], (LEAVES, LEAF, RANK), RANK ** -0.5, 0.375, ((0, 128),))
    leaf_coupling = noise(seeds[5], (LEAVES, 3, RANK, RANK), RANK ** -0.5, 0.375, ((0, 128),))
    transfer_up = draw_transfer_up(jax.random.fold_in(seeds[10], 71), 0)
    transfer_down = draw_transfer_down(jax.random.fold_in(seeds[10], 71), 0)
    node_coupling = draw_node_coupling(jax.random.fold_in(seeds[10], 71), 0)
    ridge = jnp.clip(jax.random.uniform(seeds[9], (1,), jnp.float32, 0.5, 2.0), 0.5, 2.0)
    return dict(points=points, order=order, near=near, basis_in=basis_in, basis_out=basis_out, leaf_coupling=leaf_coupling, transfer_up=transfer_up, transfer_down=transfer_down, node_coupling=node_coupling, ridge=ridge)


SIBLINGS = np.array([[1, 2, 3], [0, 2, 3], [0, 1, 3], [0, 1, 2]], dtype=np.int32)


def couple(node_hats, coupling):
    count = node_hats.shape[0]
    grouped = node_hats.reshape(count // 4, 4, node_hats.shape[1], node_hats.shape[2])
    others = grouped[:, SIBLINGS].reshape(count, 3, node_hats.shape[1], node_hats.shape[2])
    return jnp.einsum('njrs,njsc->nrc', coupling.astype(jnp.float32), others.astype(jnp.float32))


def leaf_up(leaf_items):
    return jnp.dot(leaf_items[0].T, leaf_items[1], preferred_element_type=jnp.float32).astype(jnp.bfloat16)


def leaf_out(leaf_items):
    dense_block, out_basis, values, far_rows = leaf_items
    return jnp.dot(dense_block, values, preferred_element_type=jnp.float32) + jnp.dot(out_basis, far_rows, preferred_element_type=jnp.float32)


def reference(points, order, near, basis_in, basis_out, leaf_coupling, transfer_up, transfer_down, node_coupling, ridge):
    ordered = jnp.take(points, order.astype(jnp.int32), axis=0)
    rounded = ordered.astype(jnp.bfloat16).reshape(LEAVES, LEAF, COLS)
    node_hats = [lax.map(leaf_up, (basis_in, rounded))]
    for height in range(1, LEVELS):
        stride = 4 ** height // LEAF_DEV
        lifters = transfer_up[::stride, height - 1]
        below_hats = node_hats[-1].reshape(lifters.shape[0], 4 * RANK, COLS)
        lifted = jnp.einsum('nkr,nkc->nrc', lifters.astype(jnp.float32), below_hats.astype(jnp.float32))
        node_hats.append(lifted.astype(jnp.bfloat16))
    far_terms = [couple(node_hats[0], leaf_coupling)]
    for height in range(1, LEVELS):
        stride = 4 ** height // LEAF_DEV
        far_terms.append(couple(node_hats[height], node_coupling[::stride, height - 1]))
    down_value = far_terms[LEVELS - 1]
    for height in range(LEVELS - 2, -1, -1):
        stride = 4 ** (height + 1) // LEAF_DEV
        lowers = transfer_down[::stride, height]
        parent_rows = lax.optimization_barrier(down_value.astype(jnp.bfloat16)).astype(jnp.float32)
        spread = jnp.einsum('nkr,nrc->nkc', lowers.astype(jnp.float32), parent_rows)
        down_value = far_terms[height] + spread.reshape(-1, RANK, COLS)
    lowered = down_value.astype(jnp.bfloat16)
    tree_out = lax.map(leaf_out, (near, basis_out, rounded, lowered))
    tree_out = tree_out + ridge[0] * ordered.reshape(LEAVES, LEAF, COLS)
    return jnp.zeros_like(points).at[order.astype(jnp.int32)].set(tree_out.reshape(POINTS, COLS))
```

```python
import jax
import jax.numpy as jnp
from jax import lax
from jax.experimental import pallas as pl
from jax.experimental.pallas import tpu as pltpu
from jax.sharding import PartitionSpec as P

F32 = jnp.float32
BF16 = jnp.bfloat16
MESH = pl.DeviceIdType.MESH

ROWS = 2048
LEAF = 1024
COLS = 512
RANK = 256
HALF = 256
PART = 64
TILES = ROWS // 8
LANES = COLS // 128
FLAT = ROWS * LANES
BATCH = 16
UNROLL = 64


def nt(a, b):
    return lax.dot_general(a, b, (((1,), (1,)), ((), ())), preferred_element_type=F32)


def nn(a, b):
    return jnp.dot(a, b, preferred_element_type=F32)


def row_places(order):
    local = order & (ROWS - 1)
    return ((local >> 3) << 5) + (local & 7)


def place_of(places, step, u):
    return places[step >> 1, (step & 1) * UNROLL + u]


def tree_kernel(
    order,
    ridge,
    points,
    near,
    basis_in,
    leaf_coupling,
    transfer_up,
    transfer_down,
    node_coupling,
    acc,
    low0,
    pts_v,
    near_v,
    basis_v,
    lc_v,
    up_v,
    dn1_v,
    dn2_v,
    dn3_v,
    nc_v,
    place_v,
    place_s,
    rounded,
    hat0,
    sib0,
    hat1,
    all1,
    hat2,
    all2,
    hat3,
    all3,
    far0,
    far1,
    low2,
    low1,
    load_sem,
    point_sem,
    place_sem,
    a_send,
    a_recv,
    b_send,
    b_recv,
    b2_send,
    b2_recv,
    c_send,
    c_recv,
    d_send,
    d_recv,
    e_send,
    e_recv,
    f_send,
    f_recv,
):
    gx = lax.axis_index("gx")
    gy = lax.axis_index("gy")
    gz = lax.axis_index("gz")
    x = gz // 2
    k = lax.rem(gz, 2)
    twin = (gx, gy, x * 2 + (1 - k))
    on_x = [None] + [(gx, gy, lax.rem(x + j, 4) * 2 + k) for j in (1, 2, 3)]
    on_y = [None] + [(gx, lax.rem(gy + j, 4), gz) for j in (1, 2, 3)]
    on_g = [None] + [(lax.rem(gx + j, 4), gy, gz) for j in (1, 2, 3)]

    barrier = pltpu.get_barrier_semaphore()
    for dev in [twin] + on_x[1:] + on_y[1:] + on_g[1:]:
        pl.semaphore_signal(barrier, inc=1, device_id=dev, device_id_type=MESH)

    chunk = FLAT // 4
    point_copies = [
        pltpu.make_async_copy(
            points.at[pl.ds(i * chunk, chunk)],
            pts_v.at[pl.ds(i * chunk, chunk)],
            point_sem.at[i],
        )
        for i in range(4)
    ]
    for c in point_copies:
        c.start()
    place_v[...] = row_places(order[...])
    place_copy = pltpu.make_async_copy(place_v, place_s, place_sem)
    place_copy.start()

    def rank_rows(i):
        return pl.ds(pl.multiple_of(i * RANK, RANK), RANK)

    loads = [
        pltpu.make_async_copy(basis_in, basis_v, load_sem.at[0]),
        pltpu.make_async_copy(transfer_up.at[0], up_v, load_sem.at[1]),
        pltpu.make_async_copy(near, near_v, load_sem.at[2]),
        pltpu.make_async_copy(leaf_coupling, lc_v, load_sem.at[3]),
        pltpu.make_async_copy(node_coupling.at[0], nc_v, load_sem.at[4]),
        pltpu.make_async_copy(
            transfer_down.at[0, 0, pl.ds(pl.multiple_of(k * 2 * RANK, 2 * RANK), 2 * RANK)],
            dn1_v,
            load_sem.at[5],
        ),
        pltpu.make_async_copy(transfer_down.at[0, 1, rank_rows(x)], dn2_v, load_sem.at[6]),
        pltpu.make_async_copy(transfer_down.at[0, 2, rank_rows(gy)], dn3_v, load_sem.at[7]),
    ]
    place_copy.wait()
    for c in point_copies:
        c.wait()
    for c in loads:
        c.start()

    def gather(step, _):
        for w in range(UNROLL // BATCH):
            rows = []
            for u in range(w * BATCH, (w + 1) * BATCH):
                rows.append(pts_v[pl.ds(place_of(place_s, step, u), LANES, stride=8), :])
            for u in range(w * BATCH, (w + 1) * BATCH):
                to = step * (UNROLL * LANES) + (u // 8) * 32 + (u % 8)
                acc[pl.ds(to, LANES, stride=8), :] = rows[u - w * BATCH]
        return 0

    lax.fori_loop(0, ROWS // UNROLL, gather, 0)
    acc4 = acc.reshape(TILES, LANES, 8, 128)

    def to_bf16(step, _):
        for c in range(LANES):
            block = acc4[pl.ds(step * 16, 16), c]
            rounded[pl.ds(step * 128, 128), c * 128 : (c + 1) * 128] = block.reshape(128, 128).astype(BF16)
        return 0

    lax.fori_loop(0, ROWS // 128, to_bf16, 0)

    loads[0].wait()
    for leaf in range(2):
        hat0[leaf] = lax.dot_general(
            rounded[leaf * LEAF : (leaf + 1) * LEAF],
            basis_v[leaf],
            (((0,), (0,)), ((), ())),
            preferred_element_type=F32,
        ).astype(BF16)
    pl.semaphore_wait(barrier, 10)

    mine = pl.ds(pl.multiple_of(k * HALF, HALF), HALF)
    other = pl.ds(pl.multiple_of((1 - k) * HALF, HALF), HALF)

    def remote(src, dst, send, recv, dev):
        return pltpu.make_async_remote_copy(
            src_ref=src, dst_ref=dst, send_sem=send, recv_sem=recv, device_id=dev, device_id_type=MESH
        )

    a_copies = [
        remote(hat0.at[:, rows], sib0.at[:, rows], a_send.at[i], a_recv.at[i], twin)
        for i, rows in enumerate((other, mine))
    ]
    a_copies[0].start()
    a_copies[1].start()

    gain = ridge[0]
    loads[2].wait()

    def near_chunk(i):
        leaf, q = i // 4, i % 4
        block = nn(near_v[leaf, q * 256 : (q + 1) * 256], rounded[leaf * LEAF : (leaf + 1) * LEAF])
        t = leaf * 128 + q * 32
        for c in range(LANES):
            acc4[t : t + 32, c] = acc4[t : t + 32, c] * gain + block[:, c * 128 : (c + 1) * 128].reshape(32, 8, 128)

    loads[1].wait()
    total1 = nn(hat0[0, mine], up_v[0, rank_rows(2 * k)]) + nn(hat0[1, mine], up_v[0, rank_rows(2 * k + 1)])
    near_chunk(0)
    near_chunk(1)
    remote(hat0.at[:, other], sib0.at[:, mine], a_send.at[0], a_recv.at[0], twin).wait_recv()
    sib = 1 - k
    total1 += nn(sib0[0, mine], up_v[0, rank_rows(2 * sib)]) + nn(sib0[1, mine], up_v[0, rank_rows(2 * sib + 1)])
    value1 = total1.astype(BF16)
    hat1[0:HALF] = value1
    hat1[HALF : 2 * HALF] = value1
    b_copies, b2_copies = [None], [None]
    for j in (1, 2, 3):
        start = lax.rem(x + j, 4) * PART
        b_copies.append(
            remote(
                hat1.at[pl.ds(pl.multiple_of(start, PART), PART)],
                all1.at[x, 0:PART],
                b_send.at[j - 1],
                b_recv.at[j - 1],
                on_x[j],
            )
        )
        b2_copies.append(
            remote(
                hat1.at[pl.ds(pl.multiple_of(start + PART, PART), 3 * PART)],
                all1.at[x, PART:HALF],
                b2_send.at[j - 1],
                b2_recv.at[j - 1],
                on_x[j],
            )
        )
    for j in (2, 1, 3):
        b_copies[j].start()
    for j in (2, 1, 3):
        b2_copies[j].start()

    total2 = nn(hat1[pl.ds(pl.multiple_of(x * PART, PART), PART)], up_v[1, rank_rows(x)])
    near_chunk(2)
    near_chunk(3)
    near_chunk(4)
    for j in (1, 3, 2):
        s = lax.rem(x - j + 4, 4)
        b_copies[j].wait_recv()
        total2 += nn(all1[s, 0:PART], up_v[1, rank_rows(s)])
    hat2[...] = total2.astype(BF16)
    c_copies = [None] + [
        remote(hat2, all2.at[gy], c_send.at[j - 1], c_recv.at[j - 1], on_y[j]) for j in (1, 2, 3)
    ]
    for j in (2, 1, 3):
        c_copies[j].start()

    total3 = nn(hat2[...], up_v[2, rank_rows(gy)])
    near_chunk(5)
    near_chunk(6)
    near_chunk(7)
    for j in (1, 3, 2):
        s = lax.rem(gy - j + 4, 4)
        c_copies[j].wait_recv()
        total3 += nn(all2[s], up_v[2, rank_rows(s)])
    hat3[...] = total3.astype(BF16)
    d_copies = [None] + [
        remote(hat3, all3.at[gx], d_send.at[j - 1], d_recv.at[j - 1], on_g[j]) for j in (1, 2, 3)
    ]
    for j in (2, 1, 3):
        d_copies[j].start()

    def skip(s, own):
        return jnp.where(s > own, s - 1, s)

    loads[3].wait()
    loads[4].wait()
    far2 = jnp.zeros((PART, RANK), F32)
    for j in (1, 2, 3):
        s = lax.rem(gy - j + 4, 4)
        far2 += nt(all2[s], nc_v[1, skip(s, gy)])
    a_copies[1].wait_recv()
    for leaf in range(2):
        far0[leaf] = (
            nt(hat0[1 - leaf], lc_v[leaf, 2 * k])
            + nt(sib0[0], lc_v[leaf, 1 - k])
            + nt(sib0[1], lc_v[leaf, 2 - k])
        )
    far3 = jnp.zeros((PART, RANK), F32)
    for j in (1, 3, 2):
        s = lax.rem(gx - j + 4, 4)
        d_copies[j].wait_recv()
        far3 += nt(all3[s], nc_v[2, skip(s, gx)])

    loads[7].wait()
    value2 = (far2 + nt(far3.astype(BF16), dn3_v[...])).astype(BF16)
    low2[0:PART] = value2
    e_copies = [None] + [
        remote(
            low2.at[0:PART],
            low2.at[(4 - j) * PART : (5 - j) * PART],
            e_send.at[j - 1],
            e_recv.at[j - 1],
            on_x[j],
        )
        for j in (1, 2, 3)
    ]
    for j in (2, 1, 3):
        e_copies[j].start()
    total = jnp.zeros((HALF, RANK), F32)
    for j in (1, 2, 3):
        s = lax.rem(x - j + 4, 4)
        b2_copies[j].wait_recv()
        total += nt(all1[s], nc_v[0, skip(s, x)])
    far1[...] = total
    loads[6].wait()
    for m in (0, 3, 1, 2):
        if m:
            e_copies[4 - m].wait_recv()
        value = far1[m * PART : (m + 1) * PART] + nt(low2[m * PART : (m + 1) * PART], dn2_v[...])
        to = k * HALF + lax.rem(x + m, 4) * PART
        low1[pl.ds(pl.multiple_of(to, PART), PART)] = value.astype(BF16)
    f_copy = remote(low1.at[mine], low1.at[mine], f_send, f_recv, twin)
    f_copy.start()
    loads[5].wait()

    def leaf_down(rows):
        for leaf in range(2):
            value = far0[leaf, rows] + nt(low1[rows], dn1_v[leaf * RANK : (leaf + 1) * RANK])
            low0[leaf, rows] = value.astype(BF16)

    leaf_down(mine)
    remote(low1.at[other], low1.at[other], f_send, f_recv, twin).wait_recv()
    leaf_down(other)

    for c in a_copies + b_copies[1:] + b2_copies[1:] + c_copies[1:] + d_copies[1:] + e_copies[1:] + [f_copy]:
        c.wait_send()


def leaf_kernel(order, acc, basis_out, low0, out, place_v, place_s, fin, out_v, place_sem, out_sem):
    place_v[...] = row_places(order[...])
    place_copy = pltpu.make_async_copy(place_v, place_s, place_sem)
    place_copy.start()
    acc4 = acc.reshape(TILES, LANES, 8, 128)
    fin4 = fin.reshape(TILES, LANES, 8, 128)
    for i in range(8):
        leaf, q = i // 4, i % 4
        block = nt(basis_out[leaf, q * 256 : (q + 1) * 256], low0[leaf])
        t = leaf * 128 + q * 32
        for c in range(LANES):
            fin4[t : t + 32, c] = acc4[t : t + 32, c] + block[:, c * 128 : (c + 1) * 128].reshape(32, 8, 128)
    place_copy.wait()

    def scatter(step, _):
        for w in range(UNROLL // BATCH):
            rows = []
            for u in range(w * BATCH, (w + 1) * BATCH):
                at = step * (UNROLL * LANES) + (u // 8) * 32 + (u % 8)
                rows.append(fin[pl.ds(at, LANES, stride=8), :])
            for u in range(w * BATCH, (w + 1) * BATCH):
                out_v[pl.ds(place_of(place_s, step, u), LANES, stride=8), :] = rows[u - w * BATCH]
        return 0

    lax.fori_loop(0, ROWS // UNROLL, scatter, 0)
    chunk = FLAT // 4
    copies = [
        pltpu.make_async_copy(
            out_v.at[pl.ds(i * chunk, chunk)], out.at[pl.ds(i * chunk, chunk)], out_sem.at[i]
        )
        for i in range(4)
    ]
    for c in copies:
        c.start()
    for c in copies:
        c.wait()


def on_device(
    points,
    order,
    near,
    basis_in,
    basis_out,
    leaf_coupling,
    transfer_up,
    transfer_down,
    node_coupling,
    ridge,
):
    flat_points = points.reshape(TILES, 8, LANES, 128).transpose(0, 2, 1, 3).reshape(FLAT, 128)
    order_rows = order.reshape(ROWS // 128, 128)
    vmem = pl.BlockSpec(memory_space=pltpu.VMEM)
    smem = pl.BlockSpec(memory_space=pltpu.SMEM)
    hbm = pl.BlockSpec(memory_space=pltpu.HBM)
    dma = pltpu.SemaphoreType.DMA
    acc, low0 = pl.pallas_call(
        tree_kernel,
        out_shape=(
            jax.ShapeDtypeStruct((FLAT, 128), F32),
            jax.ShapeDtypeStruct((2, COLS, RANK), BF16),
        ),
        in_specs=[vmem, smem] + [hbm] * 7,
        out_specs=(vmem, vmem),
        scratch_shapes=[
            pltpu.VMEM((FLAT, 128), F32),
            pltpu.VMEM((2, LEAF, LEAF), BF16),
            pltpu.VMEM((2, LEAF, RANK), BF16),
            pltpu.VMEM((2, 3, RANK, RANK), BF16),
            pltpu.VMEM((3, 4 * RANK, RANK), BF16),
            pltpu.VMEM((2 * RANK, RANK), BF16),
            pltpu.VMEM((RANK, RANK), BF16),
            pltpu.VMEM((RANK, RANK), BF16),
            pltpu.VMEM((3, 3, RANK, RANK), BF16),
            pltpu.VMEM((ROWS // 128, 128), jnp.int32),
            pltpu.SMEM((ROWS // 128, 128), jnp.int32),
            pltpu.VMEM((ROWS, COLS), BF16),
            pltpu.VMEM((2, COLS, RANK), BF16),
            pltpu.VMEM((2, COLS, RANK), BF16),
            pltpu.VMEM((2 * HALF, RANK), BF16),
            pltpu.VMEM((4, HALF, RANK), BF16),
            pltpu.VMEM((PART, RANK), BF16),
            pltpu.VMEM((4, PART, RANK), BF16),
            pltpu.VMEM((PART, RANK), BF16),
            pltpu.VMEM((4, PART, RANK), BF16),
            pltpu.VMEM((2, COLS, RANK), F32),
            pltpu.VMEM((HALF, RANK), F32),
            pltpu.VMEM((4 * PART, RANK), BF16),
            pltpu.VMEM((COLS, RANK), BF16),
            dma((8,)),
            dma((4,)),
            dma,
            dma((2,)),
            dma((2,)),
            dma((3,)),
            dma((3,)),
            dma((3,)),
            dma((3,)),
            dma((3,)),
            dma((3,)),
            dma((3,)),
            dma((3,)),
            dma((3,)),
            dma((3,)),
            dma,
            dma,
        ],
        compiler_params=pltpu.CompilerParams(
            collective_id=0, has_side_effects=True, vmem_limit_bytes=54 << 20
        ),
        name="tree",
    )(
        order_rows,
        ridge,
        flat_points,
        near,
        basis_in,
        leaf_coupling,
        transfer_up,
        transfer_down,
        node_coupling,
    )
    out = pl.pallas_call(
        leaf_kernel,
        out_shape=jax.ShapeDtypeStruct((FLAT, 128), F32),
        in_specs=[vmem] * 4,
        out_specs=hbm,
        scratch_shapes=[
            pltpu.VMEM((ROWS // 128, 128), jnp.int32),
            pltpu.SMEM((ROWS // 128, 128), jnp.int32),
            pltpu.VMEM((FLAT, 128), F32),
            pltpu.VMEM((FLAT, 128), F32),
            dma,
            dma((4,)),
        ],
        compiler_params=pltpu.CompilerParams(vmem_limit_bytes=24 << 20),
        name="leaves",
    )(order_rows, acc, basis_out, low0)
    return out.reshape(TILES, LANES, 8, 128).transpose(0, 2, 1, 3).reshape(ROWS, COLS)


def solution(mesh):
    placed = (
        P(("gx", "gy", "gz"), None),
        P(("gx", "gy", "gz")),
        P(("gx", "gy", "gz"), None, None),
        P(("gx", "gy", "gz"), None, None),
        P(("gx", "gy", "gz"), None, None),
        P(("gx", "gy", "gz"), None, None, None),
        P(("gx", "gy", "gz"), None, None, None),
        P(("gx", "gy", "gz"), None, None, None),
        P(("gx", "gy", "gz"), None, None, None, None),
        P(),
    )
    return jax.shard_map(
        on_device,
        mesh=mesh,
        in_specs=placed,
        out_specs=P(("gx", "gy", "gz"), None),
        check_vma=False,
    )
```

```python
import jax
import jax.numpy as jnp
from jax import lax
from jax.experimental import pallas as pl
from jax.experimental.pallas import tpu as pltpu
from jax.sharding import PartitionSpec as P

F32 = jnp.float32
BF16 = jnp.bfloat16
MESH = pl.DeviceIdType.MESH

ROWS = 2048
LEAF = 1024
COLS = 512
RANK = 256
HALF = 256
PART = 64
TILES = ROWS // 8
LANES = COLS // 128
FLAT = ROWS * LANES
WIDE = 2 * LANES
GROUP = 128
GROUPS = ROWS // GROUP
BATCH = 16


def nt(a, b):
    return lax.dot_general(a, b, (((1,), (1,)), ((), ())), preferred_element_type=F32)


def nn(a, b):
    return jnp.dot(a, b, preferred_element_type=F32)


def row_places(index, tiles):
    return (index >> 3) * (8 * tiles) + (index & 7)


def inverse_of(local):
    high, low = local >> 7, local & 127
    row_high = lax.broadcasted_iota(jnp.int32, (GROUPS, GROUP), 0)
    row_low = lax.broadcasted_iota(jnp.int32, (GROUP, GROUP), 0)
    lane = lax.broadcasted_iota(jnp.int32, (GROUPS, GROUP), 1).astype(F32)
    total = jnp.zeros((2 * GROUPS, GROUP), F32)
    for b in range(GROUPS):
        hit_high = jnp.where(row_high == high[b : b + 1], 1.0, 0.0)
        hit_low = jnp.where(row_low == low[b : b + 1], 1.0, 0.0).astype(BF16)
        values = jnp.concatenate([hit_high * float(b), hit_high * lane], axis=0).astype(BF16)
        total += nt(values, hit_low)
    return (total[:GROUPS] * float(GROUP) + total[GROUPS:]).astype(jnp.int32) & (ROWS - 1)


def move_rows(places, source, target, tiles, target_tiles, first, count):
    def step(i, _):
        for w in range(GROUP // BATCH):
            rows = []
            for u in range(w * BATCH, (w + 1) * BATCH):
                rows.append(source[pl.ds(places[i, u], tiles, stride=8), :])
            for u in range(w * BATCH, (w + 1) * BATCH):
                to = i * (GROUP * target_tiles) + (u // 8) * (8 * target_tiles) + (u % 8)
                target[pl.ds(to, tiles, stride=8), :] = rows[u - w * BATCH]
        return 0

    lax.fori_loop(first, first + count, step, 0)


def tree_kernel(
    order,
    ridge,
    points,
    near,
    basis_in,
    basis_out,
    leaf_coupling,
    transfer_up,
    transfer_down,
    node_coupling,
    turned,
    turned_basis,
    low0,
    pts_v,
    wide,
    out_basis_v,
    near_v,
    basis_v,
    lc_v,
    up_v,
    dn1_v,
    dn2_v,
    dn3_v,
    nc_v,
    order_v,
    ridge_s,
    place_v,
    place_s,
    back_v,
    back_s,
    rounded,
    hat0,
    sib0,
    hat1,
    all1,
    hat2,
    all2,
    hat3,
    all3,
    far0,
    far1,
    low2,
    low1,
    small_sem,
    load_sem,
    point_sem,
    place_sem,
    a_send,
    a_recv,
    b_send,
    b_recv,
    b2_send,
    b2_recv,
    c_send,
    c_recv,
    d_send,
    d_recv,
    e_send,
    e_recv,
    f_send,
    f_recv,
):
    gx = lax.axis_index("gx")
    gy = lax.axis_index("gy")
    gz = lax.axis_index("gz")
    x = gz // 2
    k = lax.rem(gz, 2)
    twin = (gx, gy, x * 2 + (1 - k))
    on_x = [None] + [(gx, gy, lax.rem(x + j, 4) * 2 + k) for j in (1, 2, 3)]
    on_y = [None] + [(gx, lax.rem(gy + j, 4), gz) for j in (1, 2, 3)]
    on_g = [None] + [(lax.rem(gx + j, 4), gy, gz) for j in (1, 2, 3)]

    barrier = pltpu.get_barrier_semaphore()
    for dev in [twin] + on_x[1:] + on_y[1:] + on_g[1:]:
        pl.semaphore_signal(barrier, inc=1, device_id=dev, device_id_type=MESH)

    chunk = FLAT // 4
    point_copies = [
        pltpu.make_async_copy(
            points.at[pl.ds(i * chunk, chunk)],
            pts_v.at[pl.ds(i * chunk, chunk)],
            point_sem.at[i],
        )
        for i in range(4)
    ]
    for c in point_copies:
        c.start()
    small = [
        pltpu.make_async_copy(order, order_v, small_sem.at[0]),
        pltpu.make_async_copy(ridge, ridge_s, small_sem.at[1]),
    ]
    for c in small:
        c.start()
    small[0].wait()
    local = order_v[...] & (ROWS - 1)
    place_v[...] = row_places(local, LANES)
    place_copy = pltpu.make_async_copy(place_v, place_s, place_sem.at[0])
    place_copy.start()
    back_v[...] = row_places(inverse_of(local), WIDE)
    back_copy = pltpu.make_async_copy(back_v, back_s, place_sem.at[1])
    back_copy.start()

    def rank_rows(i):
        return pl.ds(pl.multiple_of(i * RANK, RANK), RANK)

    loads = [
        pltpu.make_async_copy(basis_in, basis_v, load_sem.at[0]),
        pltpu.make_async_copy(transfer_up.at[0], up_v, load_sem.at[1]),
        pltpu.make_async_copy(near, near_v, load_sem.at[2]),
        pltpu.make_async_copy(leaf_coupling, lc_v, load_sem.at[3]),
        pltpu.make_async_copy(node_coupling.at[0], nc_v, load_sem.at[4]),
        pltpu.make_async_copy(
            transfer_down.at[0, 0, pl.ds(pl.multiple_of(k * 2 * RANK, 2 * RANK), 2 * RANK)],
            dn1_v,
            load_sem.at[5],
        ),
        pltpu.make_async_copy(transfer_down.at[0, 1, rank_rows(x)], dn2_v, load_sem.at[6]),
        pltpu.make_async_copy(transfer_down.at[0, 2, rank_rows(gy)], dn3_v, load_sem.at[7]),
        pltpu.make_async_copy(basis_out, out_basis_v, load_sem.at[8]),
    ]
    place_copy.wait()
    for c in point_copies:
        c.wait()
    for c in loads:
        c.start()

    move_rows(place_s, pts_v, wide, LANES, WIDE, 0, GROUPS)
    wide4 = wide.reshape(TILES, WIDE, 8, 128)

    def to_bf16(step, _):
        for c in range(LANES):
            block = wide4[pl.ds(step * 16, 16), c]
            rounded[pl.ds(step * 128, 128), c * 128 : (c + 1) * 128] = block.reshape(128, 128).astype(BF16)
        return 0

    lax.fori_loop(0, ROWS // 128, to_bf16, 0)

    loads[0].wait()
    mine = pl.ds(pl.multiple_of(k * HALF, HALF), HALF)
    other = pl.ds(pl.multiple_of((1 - k) * HALF, HALF), HALF)

    def remote(src, dst, send, recv, dev):
        return pltpu.make_async_remote_copy(
            src_ref=src, dst_ref=dst, send_sem=send, recv_sem=recv, device_id=dev, device_id_type=MESH
        )

    def leaf_up(columns):
        for leaf in range(2):
            hat0[leaf, columns] = lax.dot_general(
                rounded[leaf * LEAF : (leaf + 1) * LEAF, columns],
                basis_v[leaf],
                (((0,), (0,)), ((), ())),
                preferred_element_type=F32,
            ).astype(BF16)

    a_copies = [
        remote(hat0.at[:, rows], sib0.at[:, rows], a_send.at[i], a_recv.at[i], twin)
        for i, rows in enumerate((other, mine))
    ]
    leaf_up(other)
    pl.semaphore_wait(barrier, 10)
    a_copies[0].start()
    leaf_up(mine)
    a_copies[1].start()

    small[1].wait()
    gain = ridge_s[0]
    loads[2].wait()

    def near_chunk(i):
        leaf, q = i // 4, i % 4
        block = nn(near_v[leaf, q * 256 : (q + 1) * 256], rounded[leaf * LEAF : (leaf + 1) * LEAF])
        t = leaf * 128 + q * 32
        for c in range(LANES):
            wide4[t : t + 32, c] = wide4[t : t + 32, c] * gain + block[:, c * 128 : (c + 1) * 128].reshape(32, 8, 128)

    def basis_rows(leaf):
        none = jnp.zeros((32, 8, 128), F32)
        for q in range(4):
            t = leaf * 128 + q * 32
            for c in range(2):
                block = out_basis_v[leaf, q * 256 : (q + 1) * 256, c * 128 : (c + 1) * 128]
                wide4[t : t + 32, LANES + leaf * 2 + c] = block.astype(F32).reshape(32, 8, 128)
                wide4[t : t + 32, LANES + (1 - leaf) * 2 + c] = none

    def turn(first, count):
        move_rows(back_s, wide, turned, WIDE, WIDE, first, count)

    turned4 = turned.reshape(TILES, WIDE, 8, 128)

    def turned_to_bf16(first, count):
        def step(i, _):
            for c in range(LANES):
                block = turned4[pl.ds(i * 16, 16), LANES + c]
                turned_basis[pl.ds(i * 128, 128), c * 128 : (c + 1) * 128] = block.reshape(128, 128).astype(BF16)
            return 0

        lax.fori_loop(first, first + count, step, 0)

    loads[1].wait()
    total1 = nn(hat0[0, mine], up_v[0, rank_rows(2 * k)]) + nn(hat0[1, mine], up_v[0, rank_rows(2 * k + 1)])
    near_chunk(0)
    near_chunk(1)
    remote(hat0.at[:, other], sib0.at[:, mine], a_send.at[0], a_recv.at[0], twin).wait_recv()
    sib = 1 - k
    total1 += nn(sib0[0, mine], up_v[0, rank_rows(2 * sib)]) + nn(sib0[1, mine], up_v[0, rank_rows(2 * sib + 1)])
    value1 = total1.astype(BF16)
    hat1[0:HALF] = value1
    hat1[HALF : 2 * HALF] = value1
    b_copies, b2_copies = [None], [None]
    for j in (1, 2, 3):
        start = lax.rem(x + j, 4) * PART
        b_copies.append(
            remote(
                hat1.at[pl.ds(pl.multiple_of(start, PART), PART)],
                all1.at[x, 0:PART],
                b_send.at[j - 1],
                b_recv.at[j - 1],
                on_x[j],
            )
        )
        b2_copies.append(
            remote(
                hat1.at[pl.ds(pl.multiple_of(start + PART, PART), 3 * PART)],
                all1.at[x, PART:HALF],
                b2_send.at[j - 1],
                b2_recv.at[j - 1],
                on_x[j],
            )
        )
    for j in (2, 1, 3):
        b_copies[j].start()
    for j in (2, 1, 3):
        b2_copies[j].start()

    total2 = nn(hat1[pl.ds(pl.multiple_of(x * PART, PART), PART)], up_v[1, rank_rows(x)])
    for i in range(2, 8):
        near_chunk(i)
    loads[8].wait()
    basis_rows(0)
    basis_rows(1)
    back_copy.wait()
    for j in (1, 3, 2):
        s = lax.rem(x - j + 4, 4)
        b_copies[j].wait_recv()
        total2 += nn(all1[s, 0:PART], up_v[1, rank_rows(s)])
    hat2[...] = total2.astype(BF16)
    c_copies = [None] + [
        remote(hat2, all2.at[gy], c_send.at[j - 1], c_recv.at[j - 1], on_y[j]) for j in (1, 2, 3)
    ]
    for j in (2, 1, 3):
        c_copies[j].start()

    total3 = nn(hat2[...], up_v[2, rank_rows(gy)])
    turn(0, 7)
    for j in (1, 3, 2):
        s = lax.rem(gy - j + 4, 4)
        c_copies[j].wait_recv()
        total3 += nn(all2[s], up_v[2, rank_rows(s)])
    hat3[...] = total3.astype(BF16)
    d_copies = [None] + [
        remote(hat3, all3.at[gx], d_send.at[j - 1], d_recv.at[j - 1], on_g[j]) for j in (1, 2, 3)
    ]
    for j in (2, 1, 3):
        d_copies[j].start()

    def skip(s, own):
        return jnp.where(s > own, s - 1, s)

    loads[3].wait()
    loads[4].wait()
    far2 = jnp.zeros((PART, RANK), F32)
    for j in (1, 2, 3):
        s = lax.rem(gy - j + 4, 4)
        far2 += nt(all2[s], nc_v[1, skip(s, gy)])
    a_copies[1].wait_recv()
    for leaf in range(2):
        far0[leaf] = (
            nt(hat0[1 - leaf], lc_v[leaf, 2 * k])
            + nt(sib0[0], lc_v[leaf, 1 - k])
            + nt(sib0[1], lc_v[leaf, 2 - k])
        )
    turn(7, 3)
    far3 = jnp.zeros((PART, RANK), F32)
    for j in (1, 3, 2):
        s = lax.rem(gx - j + 4, 4)
        d_copies[j].wait_recv()
        far3 += nt(all3[s], nc_v[2, skip(s, gx)])

    loads[7].wait()
    value2 = (far2 + nt(far3.astype(BF16), dn3_v[...])).astype(BF16)
    low2[0:PART] = value2
    e_copies = [None] + [
        remote(
            low2.at[0:PART],
            low2.at[(4 - j) * PART : (5 - j) * PART],
            e_send.at[j - 1],
            e_recv.at[j - 1],
            on_x[j],
        )
        for j in (1, 2, 3)
    ]
    for j in (2, 1, 3):
        e_copies[j].start()
    total = jnp.zeros((HALF, RANK), F32)
    for j in (1, 2, 3):
        s = lax.rem(x - j + 4, 4)
        b2_copies[j].wait_recv()
        total += nt(all1[s], nc_v[0, skip(s, x)])
    far1[...] = total
    turn(10, 6)
    loads[6].wait()
    f_copies = []
    for m in (0, 3, 1, 2):
        if m:
            e_copies[4 - m].wait_recv()
        value = far1[m * PART : (m + 1) * PART] + nt(low2[m * PART : (m + 1) * PART], dn2_v[...])
        to = k * HALF + lax.rem(x + m, 4) * PART
        rows = pl.ds(pl.multiple_of(to, PART), PART)
        low1[rows] = value.astype(BF16)
        f_copies.append(remote(low1.at[rows], low1.at[rows], f_send.at[m], f_recv.at[m], twin))
        f_copies[-1].start()
    loads[5].wait()

    def leaf_down(rows):
        for leaf in range(2):
            value = far0[leaf, rows] + nt(low1[rows], dn1_v[leaf * RANK : (leaf + 1) * RANK])
            low0[rows, leaf * RANK : (leaf + 1) * RANK] = value.astype(BF16)

    leaf_down(mine)
    turned_to_bf16(0, 16)
    for m in (0, 3, 1, 2):
        to = (1 - k) * HALF + lax.rem(x + m, 4) * PART
        rows = pl.ds(pl.multiple_of(to, PART), PART)
        remote(low1.at[rows], low1.at[rows], f_send.at[m], f_recv.at[m], twin).wait_recv()
    leaf_down(other)

    for c in a_copies + b_copies[1:] + b2_copies[1:] + c_copies[1:] + d_copies[1:] + e_copies[1:] + f_copies:
        c.wait_send()


def leaf_kernel(turned, turned_basis, low0, out, out_v, out_sem):
    turned4 = turned.reshape(TILES, WIDE, 8, 128)
    out4 = out_v.reshape(TILES, LANES, 8, 128)
    copies = []
    for i in range(8):
        block = nt(turned_basis[i * 256 : (i + 1) * 256], low0[...])
        t = i * 32
        for c in range(LANES):
            out4[t : t + 32, c] = turned4[t : t + 32, c] + block[:, c * 128 : (c + 1) * 128].reshape(32, 8, 128)
        rows = pl.ds(i * (FLAT // 8), FLAT // 8)
        copies.append(pltpu.make_async_copy(out_v.at[rows], out.at[rows], out_sem.at[i]))
        copies[-1].start()
    for c in copies:
        c.wait()


def on_device(
    points,
    order,
    near,
    basis_in,
    basis_out,
    leaf_coupling,
    transfer_up,
    transfer_down,
    node_coupling,
    ridge,
):
    flat_points = points.reshape(TILES, 8, LANES, 128).transpose(0, 2, 1, 3).reshape(FLAT, 128)
    order_rows = order.reshape(ROWS // 128, 128)
    vmem = pl.BlockSpec(memory_space=pltpu.VMEM)
    hbm = pl.BlockSpec(memory_space=pltpu.HBM)
    dma = pltpu.SemaphoreType.DMA
    turned, turned_basis, low0 = pl.pallas_call(
        tree_kernel,
        out_shape=(
            pltpu.VMEM((2 * FLAT, 128), F32),
            pltpu.VMEM((ROWS, COLS), BF16),
            pltpu.VMEM((COLS, 2 * RANK), BF16),
        ),
        in_specs=[hbm] * 10,
        out_specs=(vmem, vmem, vmem),
        scratch_shapes=[
            pltpu.VMEM((FLAT, 128), F32),
            pltpu.VMEM((2 * FLAT, 128), F32),
            pltpu.VMEM((2, LEAF, RANK), BF16),
            pltpu.VMEM((2, LEAF, LEAF), BF16),
            pltpu.VMEM((2, LEAF, RANK), BF16),
            pltpu.VMEM((2, 3, RANK, RANK), BF16),
            pltpu.VMEM((3, 4 * RANK, RANK), BF16),
            pltpu.VMEM((2 * RANK, RANK), BF16),
            pltpu.VMEM((RANK, RANK), BF16),
            pltpu.VMEM((RANK, RANK), BF16),
            pltpu.VMEM((3, 3, RANK, RANK), BF16),
            pltpu.VMEM((ROWS // 128, 128), jnp.int32),
            pltpu.SMEM((1,), F32),
            pltpu.VMEM((ROWS // 128, 128), jnp.int32),
            pltpu.SMEM((ROWS // 128, 128), jnp.int32),
            pltpu.VMEM((ROWS // 128, 128), jnp.int32),
            pltpu.SMEM((ROWS // 128, 128), jnp.int32),
            pltpu.VMEM((ROWS, COLS), BF16),
            pltpu.VMEM((2, COLS, RANK), BF16),
            pltpu.VMEM((2, COLS, RANK), BF16),
            pltpu.VMEM((2 * HALF, RANK), BF16),
            pltpu.VMEM((4, HALF, RANK), BF16),
            pltpu.VMEM((PART, RANK), BF16),
            pltpu.VMEM((4, PART, RANK), BF16),
            pltpu.VMEM((PART, RANK), BF16),
            pltpu.VMEM((4, PART, RANK), BF16),
            pltpu.VMEM((2, COLS, RANK), F32),
            pltpu.VMEM((HALF, RANK), F32),
            pltpu.VMEM((4 * PART, RANK), BF16),
            pltpu.VMEM((COLS, RANK), BF16),
            dma((2,)),
            dma((9,)),
            dma((4,)),
            dma((2,)),
            dma((2,)),
            dma((2,)),
            dma((3,)),
            dma((3,)),
            dma((3,)),
            dma((3,)),
            dma((3,)),
            dma((3,)),
            dma((3,)),
            dma((3,)),
            dma((3,)),
            dma((3,)),
            dma((4,)),
            dma((4,)),
        ],
        compiler_params=pltpu.CompilerParams(
            collective_id=0, has_side_effects=True, vmem_limit_bytes=44 << 20
        ),
        name="tree",
    )(
        order_rows,
        ridge,
        flat_points,
        near,
        basis_in,
        basis_out,
        leaf_coupling,
        transfer_up,
        transfer_down,
        node_coupling,
    )
    out = pl.pallas_call(
        leaf_kernel,
        out_shape=jax.ShapeDtypeStruct((FLAT, 128), F32),
        in_specs=[vmem] * 3,
        out_specs=hbm,
        scratch_shapes=[pltpu.VMEM((FLAT, 128), F32), dma((8,))],
        compiler_params=pltpu.CompilerParams(vmem_limit_bytes=12 << 20),
        name="leaves",
    )(turned, turned_basis, low0)
    return out.reshape(TILES, LANES, 8, 128).transpose(0, 2, 1, 3).reshape(ROWS, COLS)


def solution(mesh):
    placed = (
        P(("gx", "gy", "gz"), None),
        P(("gx", "gy", "gz")),
        P(("gx", "gy", "gz"), None, None),
        P(("gx", "gy", "gz"), None, None),
        P(("gx", "gy", "gz"), None, None),
        P(("gx", "gy", "gz"), None, None, None),
        P(("gx", "gy", "gz"), None, None, None),
        P(("gx", "gy", "gz"), None, None, None),
        P(("gx", "gy", "gz"), None, None, None, None),
        P(),
    )
    return jax.shard_map(
        on_device,
        mesh=mesh,
        in_specs=placed,
        out_specs=P(("gx", "gy", "gz"), None),
        check_vma=False,
    )
```

```python
import jax
import jax.numpy as jnp
from jax import lax
from jax.experimental import pallas as pl
from jax.experimental.pallas import tpu as pltpu
from jax.sharding import PartitionSpec as P

F32 = jnp.float32
BF16 = jnp.bfloat16
MESH = pl.DeviceIdType.MESH

ROWS = 2048
LEAF = 1024
COLS = 512
RANK = 256
HALF = 256
PART = 64
TILES = ROWS // 8
LANES = COLS // 128
FLAT = ROWS * LANES
WIDE = 2 * LANES
GROUP = 128
GROUPS = ROWS // GROUP
BATCH = 16


def nt(a, b):
    return lax.dot_general(a, b, (((1,), (1,)), ((), ())), preferred_element_type=F32)


def nn(a, b):
    return jnp.dot(a, b, preferred_element_type=F32)


def row_places(index, tiles):
    return (index >> 3) * (8 * tiles) + (index & 7)


def inverse_of(local):
    high, low = local >> 7, local & 127
    row_high = lax.broadcasted_iota(jnp.int32, (GROUPS, GROUP), 0)
    row_low = lax.broadcasted_iota(jnp.int32, (GROUP, GROUP), 0)
    lane = lax.broadcasted_iota(jnp.int32, (GROUPS, GROUP), 1).astype(F32)
    total = jnp.zeros((2 * GROUPS, GROUP), F32)
    for b in range(GROUPS):
        hit_high = jnp.where(row_high == high[b : b + 1], 1.0, 0.0)
        hit_low = jnp.where(row_low == low[b : b + 1], 1.0, 0.0).astype(BF16)
        values = jnp.concatenate([hit_high * float(b), hit_high * lane], axis=0).astype(BF16)
        total += nt(values, hit_low)
    return (total[:GROUPS] * float(GROUP) + total[GROUPS:]).astype(jnp.int32) & (ROWS - 1)


def move_rows(places, source, target, tiles, target_tiles, first, count):
    def step(i, _):
        for w in range(GROUP // BATCH):
            rows = []
            for u in range(w * BATCH, (w + 1) * BATCH):
                rows.append(source[pl.ds(places[i, u], tiles, stride=8), :])
            for u in range(w * BATCH, (w + 1) * BATCH):
                to = i * (GROUP * target_tiles) + (u // 8) * (8 * target_tiles) + (u % 8)
                target[pl.ds(to, tiles, stride=8), :] = rows[u - w * BATCH]
        return 0

    lax.fori_loop(first, first + count, step, 0)


def tree_kernel(
    order,
    ridge,
    points,
    near,
    basis_in,
    basis_out,
    leaf_coupling,
    transfer_up,
    transfer_down,
    node_coupling,
    turned,
    turned_basis,
    low0,
    pts_v,
    wide,
    out_basis_v,
    near_v,
    basis_v,
    lc_v,
    up_v,
    dn1_v,
    dn2_v,
    dn3_v,
    nc_v,
    order_v,
    ridge_s,
    place_v,
    place_s,
    back_v,
    back_s,
    rounded,
    hat0,
    sib0,
    hat1,
    all1,
    hat2,
    all2,
    hat3,
    all3,
    far0,
    far1,
    low2,
    low1,
    small_sem,
    load_sem,
    point_sem,
    place_sem,
    a_send,
    a_recv,
    b_send,
    b_recv,
    b2_send,
    b2_recv,
    c_send,
    c_recv,
    d_send,
    d_recv,
    e_send,
    e_recv,
    f_send,
    f_recv,
):
    gx = lax.axis_index("gx")
    gy = lax.axis_index("gy")
    gz = lax.axis_index("gz")
    x = gz // 2
    k = lax.rem(gz, 2)
    twin = (gx, gy, x * 2 + (1 - k))
    on_x = [None] + [(gx, gy, lax.rem(x + j, 4) * 2 + k) for j in (1, 2, 3)]
    on_y = [None] + [(gx, lax.rem(gy + j, 4), gz) for j in (1, 2, 3)]
    on_g = [None] + [(lax.rem(gx + j, 4), gy, gz) for j in (1, 2, 3)]

    barrier = pltpu.get_barrier_semaphore()
    for dev in [twin] + on_x[1:] + on_y[1:] + on_g[1:]:
        pl.semaphore_signal(barrier, inc=1, device_id=dev, device_id_type=MESH)

    small = [
        pltpu.make_async_copy(order, order_v, small_sem.at[0]),
        pltpu.make_async_copy(ridge, ridge_s, small_sem.at[1]),
    ]
    for c in small:
        c.start()
    chunk = FLAT // 4
    point_copies = [
        pltpu.make_async_copy(
            points.at[pl.ds(i * chunk, chunk)],
            pts_v.at[pl.ds(i * chunk, chunk)],
            point_sem.at[i],
        )
        for i in range(4)
    ]
    for c in point_copies:
        c.start()
    small[0].wait()
    local = order_v[...] & (ROWS - 1)
    place_v[...] = row_places(local, LANES)
    place_copy = pltpu.make_async_copy(place_v, place_s, place_sem.at[0])
    place_copy.start()

    def rank_rows(i):
        return pl.ds(pl.multiple_of(i * RANK, RANK), RANK)

    loads = [
        pltpu.make_async_copy(basis_in, basis_v, load_sem.at[0]),
        pltpu.make_async_copy(transfer_up.at[0], up_v, load_sem.at[1]),
        pltpu.make_async_copy(near, near_v, load_sem.at[2]),
        pltpu.make_async_copy(leaf_coupling, lc_v, load_sem.at[3]),
        pltpu.make_async_copy(node_coupling.at[0], nc_v, load_sem.at[4]),
        pltpu.make_async_copy(
            transfer_down.at[0, 0, pl.ds(pl.multiple_of(k * 2 * RANK, 2 * RANK), 2 * RANK)],
            dn1_v,
            load_sem.at[5],
        ),
        pltpu.make_async_copy(transfer_down.at[0, 1, rank_rows(x)], dn2_v, load_sem.at[6]),
        pltpu.make_async_copy(transfer_down.at[0, 2, rank_rows(gy)], dn3_v, load_sem.at[7]),
        pltpu.make_async_copy(basis_out, out_basis_v, load_sem.at[8]),
    ]
    place_copy.wait()
    for c in point_copies:
        c.wait()
    for c in loads:
        c.start()

    move_rows(place_s, pts_v, wide, LANES, WIDE, 0, GROUPS)
    wide4 = wide.reshape(TILES, WIDE, 8, 128)

    def to_bf16(step, _):
        for c in range(LANES):
            block = wide4[pl.ds(step * 16, 16), c]
            rounded[pl.ds(step * 128, 128), c * 128 : (c + 1) * 128] = block.reshape(128, 128).astype(BF16)
        return 0

    lax.fori_loop(0, ROWS // 128, to_bf16, 0)

    loads[0].wait()
    mine = pl.ds(pl.multiple_of(k * HALF, HALF), HALF)
    other = pl.ds(pl.multiple_of((1 - k) * HALF, HALF), HALF)

    def remote(src, dst, send, recv, dev):
        return pltpu.make_async_remote_copy(
            src_ref=src, dst_ref=dst, send_sem=send, recv_sem=recv, device_id=dev, device_id_type=MESH
        )

    def leaf_up(columns):
        for leaf in range(2):
            hat0[leaf, columns] = lax.dot_general(
                rounded[leaf * LEAF : (leaf + 1) * LEAF, columns],
                basis_v[leaf],
                (((0,), (0,)), ((), ())),
                preferred_element_type=F32,
            ).astype(BF16)

    a_copies = [
        remote(hat0.at[:, rows], sib0.at[:, rows], a_send.at[i], a_recv.at[i], twin)
        for i, rows in enumerate((other, mine))
    ]
    leaf_up(other)
    pl.semaphore_wait(barrier, 10)
    a_copies[0].start()
    leaf_up(mine)
    a_copies[1].start()

    small[1].wait()
    gain = ridge_s[0]

    def near_chunk(i):
        leaf, q = i // 4, i % 4
        block = nn(near_v[leaf, q * 256 : (q + 1) * 256], rounded[leaf * LEAF : (leaf + 1) * LEAF])
        t = leaf * 128 + q * 32
        for c in range(LANES):
            wide4[t : t + 32, c] = wide4[t : t + 32, c] * gain + block[:, c * 128 : (c + 1) * 128].reshape(32, 8, 128)

    def basis_rows(leaf):
        none = jnp.zeros((32, 8, 128), F32)
        for q in range(4):
            t = leaf * 128 + q * 32
            for c in range(2):
                block = out_basis_v[leaf, q * 256 : (q + 1) * 256, c * 128 : (c + 1) * 128]
                wide4[t : t + 32, LANES + leaf * 2 + c] = block.astype(F32).reshape(32, 8, 128)
                wide4[t : t + 32, LANES + (1 - leaf) * 2 + c] = none

    def turn(first, count):
        move_rows(back_s, wide, turned, WIDE, WIDE, first, count)

    turned4 = turned.reshape(TILES, WIDE, 8, 128)

    def turned_to_bf16(first, count):
        def step(i, _):
            for c in range(LANES):
                block = turned4[pl.ds(i * 16, 16), LANES + c]
                turned_basis[pl.ds(i * 128, 128), c * 128 : (c + 1) * 128] = block.reshape(128, 128).astype(BF16)
            return 0

        lax.fori_loop(first, first + count, step, 0)

    loads[1].wait()
    total1 = nn(hat0[0, mine], up_v[0, rank_rows(2 * k)]) + nn(hat0[1, mine], up_v[0, rank_rows(2 * k + 1)])
    remote(hat0.at[:, other], sib0.at[:, mine], a_send.at[0], a_recv.at[0], twin).wait_recv()
    sib = 1 - k
    total1 += nn(sib0[0, mine], up_v[0, rank_rows(2 * sib)]) + nn(sib0[1, mine], up_v[0, rank_rows(2 * sib + 1)])
    value1 = total1.astype(BF16)
    hat1[0:HALF] = value1
    hat1[HALF : 2 * HALF] = value1
    b_copies, b2_copies = [None], [None]
    for j in (1, 2, 3):
        start = lax.rem(x + j, 4) * PART
        b_copies.append(
            remote(
                hat1.at[pl.ds(pl.multiple_of(start, PART), PART)],
                all1.at[x, 0:PART],
                b_send.at[j - 1],
                b_recv.at[j - 1],
                on_x[j],
            )
        )
        b2_copies.append(
            remote(
                hat1.at[pl.ds(pl.multiple_of(start + PART, PART), 3 * PART)],
                all1.at[x, PART:HALF],
                b2_send.at[j - 1],
                b2_recv.at[j - 1],
                on_x[j],
            )
        )
    for j in (2, 1, 3):
        b_copies[j].start()

    total2 = nn(hat1[pl.ds(pl.multiple_of(x * PART, PART), PART)], up_v[1, rank_rows(x)])
    back_v[...] = row_places(inverse_of(local), WIDE)
    back_copy = pltpu.make_async_copy(back_v, back_s, place_sem.at[1])
    back_copy.start()
    loads[2].wait()
    for i in range(0, 8):
        near_chunk(i)
    loads[8].wait()
    basis_rows(0)
    basis_rows(1)
    back_copy.wait()
    for j in (1, 3, 2):
        s = lax.rem(x - j + 4, 4)
        b_copies[j].wait_recv()
        total2 += nn(all1[s, 0:PART], up_v[1, rank_rows(s)])
    hat2[...] = total2.astype(BF16)
    c_copies = [None] + [
        remote(hat2, all2.at[gy], c_send.at[j - 1], c_recv.at[j - 1], on_y[j]) for j in (1, 2, 3)
    ]
    for j in (2, 1, 3):
        c_copies[j].start()
    for j in (2, 1, 3):
        b2_copies[j].start()

    total3 = nn(hat2[...], up_v[2, rank_rows(gy)])
    turn(0, 7)
    for j in (1, 3, 2):
        s = lax.rem(gy - j + 4, 4)
        c_copies[j].wait_recv()
        total3 += nn(all2[s], up_v[2, rank_rows(s)])
    hat3[...] = total3.astype(BF16)
    d_copies = [None] + [
        remote(hat3, all3.at[gx], d_send.at[j - 1], d_recv.at[j - 1], on_g[j]) for j in (1, 2, 3)
    ]
    for j in (2, 1, 3):
        d_copies[j].start()

    def skip(s, own):
        return jnp.where(s > own, s - 1, s)

    loads[3].wait()
    loads[4].wait()
    far2 = jnp.zeros((PART, RANK), F32)
    for j in (1, 2, 3):
        s = lax.rem(gy - j + 4, 4)
        far2 += nt(all2[s], nc_v[1, skip(s, gy)])
    a_copies[1].wait_recv()
    for leaf in range(2):
        far0[leaf] = (
            nt(hat0[1 - leaf], lc_v[leaf, 2 * k])
            + nt(sib0[0], lc_v[leaf, 1 - k])
            + nt(sib0[1], lc_v[leaf, 2 - k])
        )
    turn(7, 3)
    far3 = jnp.zeros((PART, RANK), F32)
    for j in (1, 3, 2):
        s = lax.rem(gx - j + 4, 4)
        d_copies[j].wait_recv()
        far3 += nt(all3[s], nc_v[2, skip(s, gx)])

    loads[7].wait()
    value2 = (far2 + nt(far3.astype(BF16), dn3_v[...])).astype(BF16)
    low2[0:PART] = value2
    e_copies = [None] + [
        remote(
            low2.at[0:PART],
            low2.at[(4 - j) * PART : (5 - j) * PART],
            e_send.at[j - 1],
            e_recv.at[j - 1],
            on_x[j],
        )
        for j in (1, 2, 3)
    ]
    for j in (2, 1, 3):
        e_copies[j].start()
    total = jnp.zeros((HALF, RANK), F32)
    for j in (1, 2, 3):
        s = lax.rem(x - j + 4, 4)
        b2_copies[j].wait_recv()
        total += nt(all1[s], nc_v[0, skip(s, x)])
    far1[...] = total
    turn(10, 6)
    loads[6].wait()
    f_copies = []
    for m in (0, 3, 1, 2):
        if m:
            e_copies[4 - m].wait_recv()
        value = far1[m * PART : (m + 1) * PART] + nt(low2[m * PART : (m + 1) * PART], dn2_v[...])
        to = k * HALF + lax.rem(x + m, 4) * PART
        rows = pl.ds(pl.multiple_of(to, PART), PART)
        low1[rows] = value.astype(BF16)
        f_copies.append(remote(low1.at[rows], low1.at[rows], f_send.at[m], f_recv.at[m], twin))
        f_copies[-1].start()
    loads[5].wait()

    def leaf_down(rows):
        for leaf in range(2):
            value = far0[leaf, rows] + nt(low1[rows], dn1_v[leaf * RANK : (leaf + 1) * RANK])
            low0[rows, leaf * RANK : (leaf + 1) * RANK] = value.astype(BF16)

    leaf_down(mine)
    turned_to_bf16(0, 16)
    for m in (0, 3, 1, 2):
        to = (1 - k) * HALF + lax.rem(x + m, 4) * PART
        rows = pl.ds(pl.multiple_of(to, PART), PART)
        remote(low1.at[rows], low1.at[rows], f_send.at[m], f_recv.at[m], twin).wait_recv()
    leaf_down(other)

    for c in a_copies + b_copies[1:] + b2_copies[1:] + c_copies[1:] + d_copies[1:] + e_copies[1:] + f_copies:
        c.wait_send()


def leaf_kernel(turned, turned_basis, low0, out, out_v, out_sem):
    turned4 = turned.reshape(TILES, WIDE, 8, 128)
    out4 = out_v.reshape(TILES, LANES, 8, 128)
    copies = []
    for i in range(8):
        block = nt(turned_basis[i * 256 : (i + 1) * 256], low0[...])
        t = i * 32
        for c in range(LANES):
            out4[t : t + 32, c] = turned4[t : t + 32, c] + block[:, c * 128 : (c + 1) * 128].reshape(32, 8, 128)
        rows = pl.ds(i * (FLAT // 8), FLAT // 8)
        copies.append(pltpu.make_async_copy(out_v.at[rows], out.at[rows], out_sem.at[i]))
        copies[-1].start()
    for c in copies:
        c.wait()


def on_device(
    points,
    order,
    near,
    basis_in,
    basis_out,
    leaf_coupling,
    transfer_up,
    transfer_down,
    node_coupling,
    ridge,
):
    flat_points = points.reshape(TILES, 8, LANES, 128).transpose(0, 2, 1, 3).reshape(FLAT, 128)
    order_rows = order.reshape(ROWS // 128, 128)
    vmem = pl.BlockSpec(memory_space=pltpu.VMEM)
    hbm = pl.BlockSpec(memory_space=pltpu.HBM)
    dma = pltpu.SemaphoreType.DMA
    turned, turned_basis, low0 = pl.pallas_call(
        tree_kernel,
        out_shape=(
            pltpu.VMEM((2 * FLAT, 128), F32),
            pltpu.VMEM((ROWS, COLS), BF16),
            pltpu.VMEM((COLS, 2 * RANK), BF16),
        ),
        in_specs=[hbm] * 10,
        out_specs=(vmem, vmem, vmem),
        scratch_shapes=[
            pltpu.VMEM((FLAT, 128), F32),
            pltpu.VMEM((2 * FLAT, 128), F32),
            pltpu.VMEM((2, LEAF, RANK), BF16),
            pltpu.VMEM((2, LEAF, LEAF), BF16),
            pltpu.VMEM((2, LEAF, RANK), BF16),
            pltpu.VMEM((2, 3, RANK, RANK), BF16),
            pltpu.VMEM((3, 4 * RANK, RANK), BF16),
            pltpu.VMEM((2 * RANK, RANK), BF16),
            pltpu.VMEM((RANK, RANK), BF16),
            pltpu.VMEM((RANK, RANK), BF16),
            pltpu.VMEM((3, 3, RANK, RANK), BF16),
            pltpu.VMEM((ROWS // 128, 128), jnp.int32),
            pltpu.SMEM((1,), F32),
            pltpu.VMEM((ROWS // 128, 128), jnp.int32),
            pltpu.SMEM((ROWS // 128, 128), jnp.int32),
            pltpu.VMEM((ROWS // 128, 128), jnp.int32),
            pltpu.SMEM((ROWS // 128, 128), jnp.int32),
            pltpu.VMEM((ROWS, COLS), BF16),
            pltpu.VMEM((2, COLS, RANK), BF16),
            pltpu.VMEM((2, COLS, RANK), BF16),
            pltpu.VMEM((2 * HALF, RANK), BF16),
            pltpu.VMEM((4, HALF, RANK), BF16),
            pltpu.VMEM((PART, RANK), BF16),
            pltpu.VMEM((4, PART, RANK), BF16),
            pltpu.VMEM((PART, RANK), BF16),
            pltpu.VMEM((4, PART, RANK), BF16),
            pltpu.VMEM((2, COLS, RANK), F32),
            pltpu.VMEM((HALF, RANK), F32),
            pltpu.VMEM((4 * PART, RANK), BF16),
            pltpu.VMEM((COLS, RANK), BF16),
            dma((2,)),
            dma((9,)),
            dma((4,)),
            dma((2,)),
            dma((2,)),
            dma((2,)),
            dma((3,)),
            dma((3,)),
            dma((3,)),
            dma((3,)),
            dma((3,)),
            dma((3,)),
            dma((3,)),
            dma((3,)),
            dma((3,)),
            dma((3,)),
            dma((4,)),
            dma((4,)),
        ],
        compiler_params=pltpu.CompilerParams(
            collective_id=0, has_side_effects=True, vmem_limit_bytes=44 << 20
        ),
        name="tree",
    )(
        order_rows,
        ridge,
        flat_points,
        near,
        basis_in,
        basis_out,
        leaf_coupling,
        transfer_up,
        transfer_down,
        node_coupling,
    )
    out = pl.pallas_call(
        leaf_kernel,
        out_shape=jax.ShapeDtypeStruct((FLAT, 128), F32),
        in_specs=[vmem] * 3,
        out_specs=hbm,
        scratch_shapes=[pltpu.VMEM((FLAT, 128), F32), dma((8,))],
        compiler_params=pltpu.CompilerParams(vmem_limit_bytes=12 << 20),
        name="leaves",
    )(turned, turned_basis, low0)
    return out.reshape(TILES, LANES, 8, 128).transpose(0, 2, 1, 3).reshape(ROWS, COLS)


def solution(mesh):
    placed = (
        P(("gx", "gy", "gz"), None),
        P(("gx", "gy", "gz")),
        P(("gx", "gy", "gz"), None, None),
        P(("gx", "gy", "gz"), None, None),
        P(("gx", "gy", "gz"), None, None),
        P(("gx", "gy", "gz"), None, None, None),
        P(("gx", "gy", "gz"), None, None, None),
        P(("gx", "gy", "gz"), None, None, None),
        P(("gx", "gy", "gz"), None, None, None, None),
        P(),
    )
    return jax.shard_map(
        on_device,
        mesh=mesh,
        in_specs=placed,
        out_specs=P(("gx", "gy", "gz"), None),
        check_vma=False,
    )
```

```python
import jax
import jax.numpy as jnp
from jax import lax
from jax.experimental import pallas as pl
from jax.experimental.pallas import tpu as pltpu
from jax.sharding import PartitionSpec as P

F32 = jnp.float32
BF16 = jnp.bfloat16
MESH = pl.DeviceIdType.MESH

ROWS = 2048
LEAF = 1024
COLS = 512
RANK = 256
HALF = 256
PART = 64
BITE = PART // 2
TILES = ROWS // 8
LANES = COLS // 128
FLAT = ROWS * LANES
WIDE = 2 * LANES
GROUP = 128
GROUPS = ROWS // GROUP
BATCH = 16
B_NEAR, C_TURN, D_TURN = 5, 4, 6


def nt(a, b):
    return lax.dot_general(a, b, (((1,), (1,)), ((), ())), preferred_element_type=F32)


def nn(a, b):
    return jnp.dot(a, b, preferred_element_type=F32)


def row_places(index, tiles):
    return (index >> 3) * (8 * tiles) + (index & 7)


def inverse_of(local):
    high, low = local >> 7, local & 127
    row_high = lax.broadcasted_iota(jnp.int32, (GROUPS, GROUP), 0)
    row_low = lax.broadcasted_iota(jnp.int32, (GROUP, GROUP), 0)
    lane = lax.broadcasted_iota(jnp.int32, (GROUPS, GROUP), 1).astype(F32)
    total = jnp.zeros((2 * GROUPS, GROUP), F32)
    for b in range(GROUPS):
        hit_high = jnp.where(row_high == high[b : b + 1], 1.0, 0.0)
        hit_low = jnp.where(row_low == low[b : b + 1], 1.0, 0.0).astype(BF16)
        values = jnp.concatenate([hit_high * float(b), hit_high * lane], axis=0).astype(BF16)
        total += nt(values, hit_low)
    return (total[:GROUPS] * float(GROUP) + total[GROUPS:]).astype(jnp.int32) & (ROWS - 1)


def move_rows(places, source, target, tiles, target_tiles, first, count):
    def step(i, _):
        for w in range(GROUP // BATCH):
            rows = []
            for u in range(w * BATCH, (w + 1) * BATCH):
                rows.append(source[pl.ds(places[i, u], tiles, stride=8), :])
            for u in range(w * BATCH, (w + 1) * BATCH):
                to = i * (GROUP * target_tiles) + (u // 8) * (8 * target_tiles) + (u % 8)
                target[pl.ds(to, tiles, stride=8), :] = rows[u - w * BATCH]
        return 0

    lax.fori_loop(first, first + count, step, 0)


def tree_kernel(
    order,
    points,
    near,
    basis_in,
    basis_out,
    leaf_coupling,
    transfer_up,
    transfer_down,
    node_coupling,
    turned,
    turned_basis,
    low0,
    pts_v,
    wide,
    out_basis_v,
    near_v,
    basis_v,
    lc_v,
    up_v,
    dn1_v,
    dn2_v,
    dn3_v,
    nc_v,
    order_v,
    place_v,
    place_s,
    back_v,
    back_s,
    rounded,
    hat0,
    sib0,
    hat1,
    all1,
    hat2,
    all2,
    hat3,
    all3,
    far0,
    far1,
    low2,
    low1,
    order_sem,
    load_sem,
    point_sem,
    place_sem,
    a_send,
    a_recv,
    b_send,
    b_recv,
    b2_send,
    b2_recv,
    c_send,
    c_recv,
    d_send,
    d_recv,
    e_send,
    e_recv,
    f_send,
    f_recv,
):
    gx = lax.axis_index("gx")
    gy = lax.axis_index("gy")
    gz = lax.axis_index("gz")
    x = gz // 2
    k = lax.rem(gz, 2)
    twin = (gx, gy, x * 2 + (1 - k))
    on_x = [None] + [(gx, gy, lax.rem(x + j, 4) * 2 + k) for j in (1, 2, 3)]
    on_y = [None] + [(gx, lax.rem(gy + j, 4), gz) for j in (1, 2, 3)]
    on_g = [None] + [(lax.rem(gx + j, 4), gy, gz) for j in (1, 2, 3)]

    order_copy = pltpu.make_async_copy(order, order_v, order_sem)
    order_copy.start()
    chunk = FLAT // 4
    point_copies = [
        pltpu.make_async_copy(
            points.at[pl.ds(i * chunk, chunk)],
            pts_v.at[pl.ds(i * chunk, chunk)],
            point_sem.at[i],
        )
        for i in range(4)
    ]
    for c in point_copies:
        c.start()
    barrier = pltpu.get_barrier_semaphore()
    for dev in [twin] + on_x[1:] + on_y[1:] + on_g[1:]:
        pl.semaphore_signal(barrier, inc=1, device_id=dev, device_id_type=MESH)

    order_copy.wait()
    local = order_v[...] & (ROWS - 1)
    place_v[...] = row_places(local, LANES)
    place_copy = pltpu.make_async_copy(place_v, place_s, place_sem.at[0])
    place_copy.start()

    def rank_rows(i):
        return pl.ds(pl.multiple_of(i * RANK, RANK), RANK)

    loads = [
        pltpu.make_async_copy(basis_in, basis_v, load_sem.at[0]),
        pltpu.make_async_copy(transfer_up.at[0], up_v, load_sem.at[1]),
        pltpu.make_async_copy(near, near_v, load_sem.at[2]),
        pltpu.make_async_copy(leaf_coupling, lc_v, load_sem.at[3]),
        pltpu.make_async_copy(node_coupling.at[0], nc_v, load_sem.at[4]),
        pltpu.make_async_copy(
            transfer_down.at[0, 0, pl.ds(pl.multiple_of(k * 2 * RANK, 2 * RANK), 2 * RANK)],
            dn1_v,
            load_sem.at[5],
        ),
        pltpu.make_async_copy(transfer_down.at[0, 1, rank_rows(x)], dn2_v, load_sem.at[6]),
        pltpu.make_async_copy(transfer_down.at[0, 2, rank_rows(gy)], dn3_v, load_sem.at[7]),
        pltpu.make_async_copy(basis_out, out_basis_v, load_sem.at[8]),
    ]
    place_copy.wait()
    for c in point_copies:
        c.wait()
    for c in loads:
        c.start()

    move_rows(place_s, pts_v, wide, LANES, WIDE, 0, GROUPS)
    wide4 = wide.reshape(TILES, WIDE, 8, 128)

    def to_bf16(step, _):
        for c in range(LANES):
            block = wide4[pl.ds(step * 16, 16), c]
            rounded[pl.ds(step * 128, 128), c * 128 : (c + 1) * 128] = block.reshape(128, 128).astype(BF16)
        return 0

    lax.fori_loop(0, ROWS // 128, to_bf16, 0)

    loads[0].wait()
    mine = pl.ds(pl.multiple_of(k * HALF, HALF), HALF)
    other = pl.ds(pl.multiple_of((1 - k) * HALF, HALF), HALF)

    def remote(src, dst, send, recv, dev):
        return pltpu.make_async_remote_copy(
            src_ref=src, dst_ref=dst, send_sem=send, recv_sem=recv, device_id=dev, device_id_type=MESH
        )

    def leaf_up(leaf, columns):
        hat0[leaf, columns] = lax.dot_general(
            rounded[leaf * LEAF : (leaf + 1) * LEAF, columns],
            basis_v[leaf],
            (((0,), (0,)), ((), ())),
            preferred_element_type=F32,
        ).astype(BF16)

    a_copies = [
        remote(hat0.at[0, other], sib0.at[0, other], a_send.at[0], a_recv.at[0], twin),
        remote(hat0.at[1, other], sib0.at[1, other], a_send.at[1], a_recv.at[1], twin),
        remote(hat0.at[:, mine], sib0.at[:, mine], a_send.at[2], a_recv.at[2], twin),
    ]
    leaf_up(0, other)
    pl.semaphore_wait(barrier, 10)
    a_copies[0].start()
    leaf_up(1, other)
    a_copies[1].start()
    leaf_up(0, mine)
    leaf_up(1, mine)
    a_copies[2].start()

    def near_chunk(i):
        leaf, q = i // 4, i % 4
        block = nn(near_v[leaf, q * 256 : (q + 1) * 256], rounded[leaf * LEAF : (leaf + 1) * LEAF])
        t = leaf * 128 + q * 32
        for c in range(LANES):
            wide4[t : t + 32, c] = block[:, c * 128 : (c + 1) * 128].reshape(32, 8, 128)

    def basis_rows(leaf):
        none = jnp.zeros((32, 8, 128), F32)
        for q in range(4):
            t = leaf * 128 + q * 32
            for c in range(2):
                block = out_basis_v[leaf, q * 256 : (q + 1) * 256, c * 128 : (c + 1) * 128]
                wide4[t : t + 32, LANES + leaf * 2 + c] = block.astype(F32).reshape(32, 8, 128)
                wide4[t : t + 32, LANES + (1 - leaf) * 2 + c] = none

    def turn(first, count):
        move_rows(back_s, wide, turned, WIDE, WIDE, first, count)

    turned4 = turned.reshape(TILES, WIDE, 8, 128)

    def turned_to_bf16(first, count):
        def step(i, _):
            for c in range(LANES):
                block = turned4[pl.ds(i * 16, 16), LANES + c]
                turned_basis[pl.ds(i * 128, 128), c * 128 : (c + 1) * 128] = block.reshape(128, 128).astype(BF16)
            return 0

        lax.fori_loop(first, first + count, step, 0)

    def bites(kind):
        return [kind[j][h] for h in (0, 1) for j in (2, 1, 3)]

    def skip(s, own):
        return jnp.where(s > own, s - 1, s)

    def before(own, j):
        return lax.rem(own - j + 4, 4)

    def spread(source, target, send, recv, where):
        return [None] + [
            [
                remote(
                    source.at[h * BITE : (h + 1) * BITE],
                    target.at[h * BITE : (h + 1) * BITE],
                    send.at[j - 1, h],
                    recv.at[j - 1, h],
                    where[j],
                )
                for h in (0, 1)
            ]
            for j in (1, 2, 3)
        ]

    loads[1].wait()
    total1 = nn(hat0[0, mine], up_v[0, rank_rows(2 * k)]) + nn(hat0[1, mine], up_v[0, rank_rows(2 * k + 1)])
    back_v[...] = row_places(inverse_of(local), WIDE)
    back_copy = pltpu.make_async_copy(back_v, back_s, place_sem.at[1])
    back_copy.start()
    sib = 1 - k
    for leaf in range(2):
        remote(
            hat0.at[leaf, other], sib0.at[leaf, mine], a_send.at[leaf], a_recv.at[leaf], twin
        ).wait_recv()
        total1 += nn(sib0[leaf, mine], up_v[0, rank_rows(2 * sib + leaf)])
    value1 = total1.astype(BF16)
    hat1[0:HALF] = value1
    hat1[HALF : 2 * HALF] = value1
    b_copies, b2_copies = [None], [None]
    for j in (1, 2, 3):
        start = lax.rem(x + j, 4) * PART
        b_copies.append(
            [
                remote(
                    hat1.at[pl.ds(pl.multiple_of(start + h * BITE, BITE), BITE)],
                    all1.at[x, h * BITE : (h + 1) * BITE],
                    b_send.at[j - 1, h],
                    b_recv.at[j - 1, h],
                    on_x[j],
                )
                for h in (0, 1)
            ]
        )
        b2_copies.append(
            remote(
                hat1.at[pl.ds(pl.multiple_of(start + PART, PART), 3 * PART)],
                all1.at[x, PART:HALF],
                b2_send.at[j - 1],
                b2_recv.at[j - 1],
                on_x[j],
            )
        )
    for c in bites(b_copies):
        c.start()

    total2 = nn(hat1[pl.ds(pl.multiple_of(x * PART, PART), PART)], up_v[1, rank_rows(x)])
    loads[2].wait()
    for i in range(B_NEAR):
        near_chunk(i)
    c_copies = spread(hat2, all2.at[gy], c_send, c_recv, on_y)
    for h in (0, 1):
        rows = slice(h * BITE, (h + 1) * BITE)
        part = total2[rows]
        for j in (1, 3, 2):
            s = before(x, j)
            b_copies[j][h].wait_recv()
            part += nn(all1[s, rows], up_v[1, rank_rows(s)])
        hat2[rows] = part.astype(BF16)
        for j in (2, 1, 3):
            c_copies[j][h].start()
    for j in (2, 1, 3):
        b2_copies[j].start()

    total3 = nn(hat2[...], up_v[2, rank_rows(gy)])
    for i in range(B_NEAR, 8):
        near_chunk(i)
    loads[8].wait()
    basis_rows(0)
    basis_rows(1)
    back_copy.wait()
    turn(0, C_TURN)
    d_copies = spread(hat3, all3.at[gx], d_send, d_recv, on_g)
    for h in (0, 1):
        rows = slice(h * BITE, (h + 1) * BITE)
        part = total3[rows]
        for j in (1, 3, 2):
            s = before(gy, j)
            c_copies[j][h].wait_recv()
            part += nn(all2[s, rows], up_v[2, rank_rows(s)])
        hat3[rows] = part.astype(BF16)
        for j in (2, 1, 3):
            d_copies[j][h].start()

    loads[3].wait()
    loads[4].wait()
    far2 = jnp.zeros((PART, RANK), F32)
    for j in (1, 2, 3):
        s = before(gy, j)
        far2 += nt(all2[s], nc_v[1, skip(s, gy)])
    a_copies[2].wait_recv()
    for leaf in range(2):
        far0[leaf] = (
            nt(hat0[1 - leaf], lc_v[leaf, 2 * k])
            + nt(sib0[0], lc_v[leaf, 1 - k])
            + nt(sib0[1], lc_v[leaf, 2 - k])
        )
    turn(C_TURN, D_TURN)
    loads[7].wait()

    e_copies = [None] + [
        [
            remote(
                low2.at[h * BITE : (h + 1) * BITE],
                low2.at[(4 - j) * PART + h * BITE : (4 - j) * PART + (h + 1) * BITE],
                e_send.at[j - 1, h],
                e_recv.at[j - 1, h],
                on_x[j],
            )
            for h in (0, 1)
        ]
        for j in (1, 2, 3)
    ]
    for h in (0, 1):
        rows = slice(h * BITE, (h + 1) * BITE)
        far3 = jnp.zeros((BITE, RANK), F32)
        for j in (1, 3, 2):
            s = before(gx, j)
            d_copies[j][h].wait_recv()
            far3 += nt(all3[s, rows], nc_v[2, skip(s, gx)])
        low2[rows] = (far2[rows] + nt(far3.astype(BF16), dn3_v[...])).astype(BF16)
        for j in (2, 1, 3):
            e_copies[j][h].start()
    total = jnp.zeros((HALF, RANK), F32)
    for j in (1, 2, 3):
        s = before(x, j)
        b2_copies[j].wait_recv()
        total += nt(all1[s], nc_v[0, skip(s, x)])
    far1[...] = total
    turn(C_TURN + D_TURN, GROUPS - C_TURN - D_TURN)
    turned_to_bf16(0, GROUPS)
    loads[6].wait()
    f_copies = []

    def half_rows(core, m, first):
        return core * HALF + lax.rem(x + m, 4) * PART + first

    def low1_block(m, first, count):
        at = m * PART + first
        value = far1[at : at + count] + nt(low2[at : at + count], dn2_v[...])
        rows = pl.ds(pl.multiple_of(half_rows(k, m, first), BITE), count)
        low1[rows] = value.astype(BF16)
        n = len(f_copies)
        f_copies.append(remote(low1.at[rows], low1.at[rows], f_send.at[n], f_recv.at[n], twin))
        f_copies[-1].start()

    blocks = [(0, 0, PART)] + [(m, h * BITE, BITE) for h in (0, 1) for m in (3, 1, 2)]
    for m, first, count in blocks:
        if m:
            e_copies[4 - m][first // BITE].wait_recv()
        low1_block(m, first, count)
    loads[5].wait()

    def leaf_down(rows):
        for leaf in range(2):
            value = far0[leaf, rows] + nt(low1[rows], dn1_v[leaf * RANK : (leaf + 1) * RANK])
            low0[rows, leaf * RANK : (leaf + 1) * RANK] = value.astype(BF16)

    leaf_down(mine)
    for n, (m, first, count) in enumerate(blocks):
        rows = pl.ds(pl.multiple_of(half_rows(1 - k, m, first), BITE), count)
        remote(low1.at[rows], low1.at[rows], f_send.at[n], f_recv.at[n], twin).wait_recv()
    leaf_down(other)

    for c in a_copies + b2_copies[1:] + f_copies:
        c.wait_send()
    for kind in (b_copies, c_copies, d_copies, e_copies):
        for c in bites(kind):
            c.wait_send()


def leaf_kernel(ridge, turned, turned_basis, low0, points, out, out_v, out_sem):
    gain = ridge[0]
    points4 = points.reshape(TILES, LANES, 8, 128)
    turned4 = turned.reshape(TILES, WIDE, 8, 128)
    out4 = out_v.reshape(TILES, LANES, 8, 128)
    copies = []
    for i in range(8):
        block = nt(turned_basis[i * 256 : (i + 1) * 256], low0[...])
        t = i * 32
        for c in range(LANES):
            fixed = turned4[t : t + 32, c] + points4[t : t + 32, c] * gain
            out4[t : t + 32, c] = fixed + block[:, c * 128 : (c + 1) * 128].reshape(32, 8, 128)
        rows = pl.ds(i * (FLAT // 8), FLAT // 8)
        copies.append(pltpu.make_async_copy(out_v.at[rows], out.at[rows], out_sem.at[i]))
        copies[-1].start()
    for c in copies:
        c.wait()


def on_device(
    points,
    order,
    near,
    basis_in,
    basis_out,
    leaf_coupling,
    transfer_up,
    transfer_down,
    node_coupling,
    ridge,
):
    flat_points = points.reshape(TILES, 8, LANES, 128).transpose(0, 2, 1, 3).reshape(FLAT, 128)
    order_rows = order.reshape(ROWS // 128, 128)
    vmem = pl.BlockSpec(memory_space=pltpu.VMEM)
    hbm = pl.BlockSpec(memory_space=pltpu.HBM)
    dma = pltpu.SemaphoreType.DMA
    turned, turned_basis, low0, held_points = pl.pallas_call(
        tree_kernel,
        out_shape=(
            pltpu.VMEM((2 * FLAT, 128), F32),
            pltpu.VMEM((ROWS, COLS), BF16),
            pltpu.VMEM((COLS, 2 * RANK), BF16),
            pltpu.VMEM((FLAT, 128), F32),
        ),
        in_specs=[hbm] * 9,
        out_specs=(vmem, vmem, vmem, vmem),
        scratch_shapes=[
            pltpu.VMEM((2 * FLAT, 128), F32),
            pltpu.VMEM((2, LEAF, RANK), BF16),
            pltpu.VMEM((2, LEAF, LEAF), BF16),
            pltpu.VMEM((2, LEAF, RANK), BF16),
            pltpu.VMEM((2, 3, RANK, RANK), BF16),
            pltpu.VMEM((3, 4 * RANK, RANK), BF16),
            pltpu.VMEM((2 * RANK, RANK), BF16),
            pltpu.VMEM((RANK, RANK), BF16),
            pltpu.VMEM((RANK, RANK), BF16),
            pltpu.VMEM((3, 3, RANK, RANK), BF16),
            pltpu.VMEM((ROWS // 128, 128), jnp.int32),
            pltpu.VMEM((ROWS // 128, 128), jnp.int32),
            pltpu.SMEM((ROWS // 128, 128), jnp.int32),
            pltpu.VMEM((ROWS // 128, 128), jnp.int32),
            pltpu.SMEM((ROWS // 128, 128), jnp.int32),
            pltpu.VMEM((ROWS, COLS), BF16),
            pltpu.VMEM((2, COLS, RANK), BF16),
            pltpu.VMEM((2, COLS, RANK), BF16),
            pltpu.VMEM((2 * HALF, RANK), BF16),
            pltpu.VMEM((4, HALF, RANK), BF16),
            pltpu.VMEM((PART, RANK), BF16),
            pltpu.VMEM((4, PART, RANK), BF16),
            pltpu.VMEM((PART, RANK), BF16),
            pltpu.VMEM((4, PART, RANK), BF16),
            pltpu.VMEM((2, COLS, RANK), F32),
            pltpu.VMEM((HALF, RANK), F32),
            pltpu.VMEM((4 * PART, RANK), BF16),
            pltpu.VMEM((COLS, RANK), BF16),
            dma,
            dma((9,)),
            dma((4,)),
            dma((2,)),
            dma((3,)),
            dma((3,)),
            dma((3, 2)),
            dma((3, 2)),
            dma((3,)),
            dma((3,)),
            dma((3, 2)),
            dma((3, 2)),
            dma((3, 2)),
            dma((3, 2)),
            dma((3, 2)),
            dma((3, 2)),
            dma((7,)),
            dma((7,)),
        ],
        compiler_params=pltpu.CompilerParams(
            collective_id=0, has_side_effects=True, vmem_limit_bytes=40 << 20
        ),
        name="tree",
    )(
        order_rows,
        flat_points,
        near,
        basis_in,
        basis_out,
        leaf_coupling,
        transfer_up,
        transfer_down,
        node_coupling,
    )
    out = pl.pallas_call(
        leaf_kernel,
        out_shape=jax.ShapeDtypeStruct((FLAT, 128), F32),
        in_specs=[pl.BlockSpec(memory_space=pltpu.SMEM)] + [vmem] * 4,
        out_specs=hbm,
        scratch_shapes=[pltpu.VMEM((FLAT, 128), F32), dma((8,))],
        compiler_params=pltpu.CompilerParams(vmem_limit_bytes=12 << 20),
        name="leaves",
    )(ridge, turned, turned_basis, low0, held_points)
    return out.reshape(TILES, LANES, 8, 128).transpose(0, 2, 1, 3).reshape(ROWS, COLS)


def solution(mesh):
    placed = (
        P(("gx", "gy", "gz"), None),
        P(("gx", "gy", "gz")),
        P(("gx", "gy", "gz"), None, None),
        P(("gx", "gy", "gz"), None, None),
        P(("gx", "gy", "gz"), None, None),
        P(("gx", "gy", "gz"), None, None, None),
        P(("gx", "gy", "gz"), None, None, None),
        P(("gx", "gy", "gz"), None, None, None),
        P(("gx", "gy", "gz"), None, None, None, None),
        P(),
    )
    return jax.shard_map(
        on_device,
        mesh=mesh,
        in_specs=placed,
        out_specs=P(("gx", "gy", "gz"), None),
        check_vma=False,
    )
```

```python
import jax
import jax.numpy as jnp
from jax import lax
from jax.experimental import pallas as pl
from jax.experimental.pallas import tpu as pltpu
from jax.sharding import PartitionSpec as P

F32 = jnp.float32
BF16 = jnp.bfloat16
MESH = pl.DeviceIdType.MESH

ROWS = 2048
LEAF = 1024
COLS = 512
RANK = 256
HALF = 256
PART = 64
BITE = PART // 2
TILES = ROWS // 8
LANES = COLS // 128
FLAT = ROWS * LANES
WIDE = 2 * LANES
GROUP = 128
GROUPS = ROWS // GROUP
BATCH = 16
B_NEAR, C_TURN, D_TURN = 5, 4, 6


def nt(a, b):
    return lax.dot_general(a, b, (((1,), (1,)), ((), ())), preferred_element_type=F32)


def nn(a, b):
    return jnp.dot(a, b, preferred_element_type=F32)


def row_places(index, tiles):
    return (index >> 3) * (8 * tiles) + (index & 7)


def inverse_of(local):
    high, low = local >> 7, local & 127
    row_high = lax.broadcasted_iota(jnp.int32, (GROUPS, GROUP), 0)
    row_low = lax.broadcasted_iota(jnp.int32, (GROUP, GROUP), 0)
    lane = lax.broadcasted_iota(jnp.int32, (GROUPS, GROUP), 1).astype(F32)
    total = jnp.zeros((2 * GROUPS, GROUP), F32)
    for b in range(GROUPS):
        hit_high = jnp.where(row_high == high[b : b + 1], 1.0, 0.0)
        hit_low = jnp.where(row_low == low[b : b + 1], 1.0, 0.0).astype(BF16)
        values = jnp.concatenate([hit_high * float(b), hit_high * lane], axis=0).astype(BF16)
        total += nt(values, hit_low)
    return (total[:GROUPS] * float(GROUP) + total[GROUPS:]).astype(jnp.int32) & (ROWS - 1)


def move_rows(places, source, target, tiles, target_tiles, first, count):
    def step(i, _):
        for w in range(GROUP // BATCH):
            rows = []
            for u in range(w * BATCH, (w + 1) * BATCH):
                rows.append(source[pl.ds(places[i, u], tiles, stride=8), :])
            for u in range(w * BATCH, (w + 1) * BATCH):
                to = i * (GROUP * target_tiles) + (u // 8) * (8 * target_tiles) + (u % 8)
                target[pl.ds(to, tiles, stride=8), :] = rows[u - w * BATCH]
        return 0

    lax.fori_loop(first, first + count, step, 0)


def tree_kernel(
    order,
    points,
    near,
    basis_in,
    basis_out,
    leaf_coupling,
    transfer_up,
    transfer_down,
    node_coupling,
    turned,
    turned_basis,
    low0,
    pts_v,
    wide,
    out_basis_v,
    near_v,
    basis_v,
    lc_v,
    up_v,
    dn1_v,
    dn2_v,
    dn3_v,
    nc_v,
    order_v,
    place_v,
    place_s,
    back_v,
    back_s,
    rounded,
    hat0,
    sib0,
    hat1,
    all1,
    hat2,
    all2,
    hat3,
    all3,
    far0,
    far1,
    low2,
    low1,
    order_sem,
    load_sem,
    point_sem,
    place_sem,
    a_send,
    a_recv,
    b_send,
    b_recv,
    b2_send,
    b2_recv,
    c_send,
    c_recv,
    d_send,
    d_recv,
    e_send,
    e_recv,
    f_send,
    f_recv,
):
    gx = lax.axis_index("gx")
    gy = lax.axis_index("gy")
    gz = lax.axis_index("gz")
    x = gz // 2
    k = lax.rem(gz, 2)
    twin = (gx, gy, x * 2 + (1 - k))
    on_x = [None] + [(gx, gy, lax.rem(x + j, 4) * 2 + k) for j in (1, 2, 3)]
    on_y = [None] + [(gx, lax.rem(gy + j, 4), gz) for j in (1, 2, 3)]
    on_g = [None] + [(lax.rem(gx + j, 4), gy, gz) for j in (1, 2, 3)]

    order_copy = pltpu.make_async_copy(order, order_v, order_sem)
    order_copy.start()
    chunk = FLAT // 4
    point_copies = [
        pltpu.make_async_copy(
            points.at[pl.ds(i * chunk, chunk)],
            pts_v.at[pl.ds(i * chunk, chunk)],
            point_sem.at[i],
        )
        for i in range(4)
    ]
    for c in point_copies:
        c.start()
    barrier = pltpu.get_barrier_semaphore()
    for dev in [twin] + on_x[1:] + on_y[1:] + on_g[1:]:
        pl.semaphore_signal(barrier, inc=1, device_id=dev, device_id_type=MESH)

    order_copy.wait()
    local = order_v[...] & (ROWS - 1)
    place_v[...] = row_places(local, LANES)
    place_copy = pltpu.make_async_copy(place_v, place_s, place_sem.at[0])
    place_copy.start()

    def rank_rows(i):
        return pl.ds(pl.multiple_of(i * RANK, RANK), RANK)

    loads = [
        pltpu.make_async_copy(basis_in, basis_v, load_sem.at[0]),
        pltpu.make_async_copy(transfer_up.at[0], up_v, load_sem.at[1]),
        pltpu.make_async_copy(near, near_v, load_sem.at[2]),
        pltpu.make_async_copy(leaf_coupling, lc_v, load_sem.at[3]),
        pltpu.make_async_copy(node_coupling.at[0], nc_v, load_sem.at[4]),
        pltpu.make_async_copy(
            transfer_down.at[0, 0, pl.ds(pl.multiple_of(k * 2 * RANK, 2 * RANK), 2 * RANK)],
            dn1_v,
            load_sem.at[5],
        ),
        pltpu.make_async_copy(transfer_down.at[0, 1, rank_rows(x)], dn2_v, load_sem.at[6]),
        pltpu.make_async_copy(transfer_down.at[0, 2, rank_rows(gy)], dn3_v, load_sem.at[7]),
        pltpu.make_async_copy(basis_out, out_basis_v, load_sem.at[8]),
    ]
    place_copy.wait()
    for c in point_copies:
        c.wait()
    for c in loads:
        c.start()

    move_rows(place_s, pts_v, wide, LANES, WIDE, 0, GROUPS)
    wide4 = wide.reshape(TILES, WIDE, 8, 128)

    def to_bf16(core):
        def step(i, _):
            for tile in range(LANES // 2):
                c = core * (LANES // 2) + tile
                block = wide4[pl.ds(i * 32, 32), c]
                lanes = pl.ds(pl.multiple_of(c * 128, 128), 128)
                rounded[pl.ds(i * 256, 256), lanes] = block.reshape(256, 128).astype(BF16)
            return 0

        lax.fori_loop(0, ROWS // 256, step, 0)

    to_bf16(1 - k)

    loads[0].wait()
    mine = pl.ds(pl.multiple_of(k * HALF, HALF), HALF)
    other = pl.ds(pl.multiple_of((1 - k) * HALF, HALF), HALF)

    def remote(src, dst, send, recv, dev):
        return pltpu.make_async_remote_copy(
            src_ref=src, dst_ref=dst, send_sem=send, recv_sem=recv, device_id=dev, device_id_type=MESH
        )

    def leaf_up(leaf, columns):
        hat0[leaf, columns] = lax.dot_general(
            rounded[leaf * LEAF : (leaf + 1) * LEAF, columns],
            basis_v[leaf],
            (((0,), (0,)), ((), ())),
            preferred_element_type=F32,
        ).astype(BF16)

    a_copies = [
        remote(hat0.at[0, other], sib0.at[0, other], a_send.at[0], a_recv.at[0], twin),
        remote(hat0.at[1, other], sib0.at[1, other], a_send.at[1], a_recv.at[1], twin),
        remote(hat0.at[:, mine], sib0.at[:, mine], a_send.at[2], a_recv.at[2], twin),
    ]
    leaf_up(0, other)
    pl.semaphore_wait(barrier, 10)
    a_copies[0].start()
    leaf_up(1, other)
    a_copies[1].start()
    to_bf16(k)
    leaf_up(0, mine)
    leaf_up(1, mine)
    a_copies[2].start()

    def near_chunk(i):
        leaf, q = i // 4, i % 4
        block = nn(near_v[leaf, q * 256 : (q + 1) * 256], rounded[leaf * LEAF : (leaf + 1) * LEAF])
        t = leaf * 128 + q * 32
        for c in range(LANES):
            wide4[t : t + 32, c] = block[:, c * 128 : (c + 1) * 128].reshape(32, 8, 128)

    def basis_rows(leaf):
        none = jnp.zeros((32, 8, 128), F32)
        for q in range(4):
            t = leaf * 128 + q * 32
            for c in range(2):
                block = out_basis_v[leaf, q * 256 : (q + 1) * 256, c * 128 : (c + 1) * 128]
                wide4[t : t + 32, LANES + leaf * 2 + c] = block.astype(F32).reshape(32, 8, 128)
                wide4[t : t + 32, LANES + (1 - leaf) * 2 + c] = none

    def turn(first, count):
        move_rows(back_s, wide, turned, WIDE, WIDE, first, count)

    turned4 = turned.reshape(TILES, WIDE, 8, 128)

    def turned_to_bf16(first, count):
        def step(i, _):
            for c in range(LANES):
                block = turned4[pl.ds(i * 16, 16), LANES + c]
                turned_basis[pl.ds(i * 128, 128), c * 128 : (c + 1) * 128] = block.reshape(128, 128).astype(BF16)
            return 0

        lax.fori_loop(first, first + count, step, 0)

    def bites(kind):
        return [kind[j][h] for h in (0, 1) for j in (2, 1, 3)]

    def skip(s, own):
        return jnp.where(s > own, s - 1, s)

    def before(own, j):
        return lax.rem(own - j + 4, 4)

    def spread(source, target, send, recv, where):
        return [None] + [
            [
                remote(
                    source.at[h * BITE : (h + 1) * BITE],
                    target.at[h * BITE : (h + 1) * BITE],
                    send.at[j - 1, h],
                    recv.at[j - 1, h],
                    where[j],
                )
                for h in (0, 1)
            ]
            for j in (1, 2, 3)
        ]

    loads[1].wait()
    total1 = nn(hat0[0, mine], up_v[0, rank_rows(2 * k)]) + nn(hat0[1, mine], up_v[0, rank_rows(2 * k + 1)])
    sib = 1 - k
    for leaf in range(2):
        remote(
            hat0.at[leaf, other], sib0.at[leaf, mine], a_send.at[leaf], a_recv.at[leaf], twin
        ).wait_recv()
        total1 += nn(sib0[leaf, mine], up_v[0, rank_rows(2 * sib + leaf)])
    value1 = total1.astype(BF16)
    hat1[0:HALF] = value1
    hat1[HALF : 2 * HALF] = value1
    b_copies, b2_copies = [None], [None]
    for j in (1, 2, 3):
        start = lax.rem(x + j, 4) * PART
        b_copies.append(
            [
                remote(
                    hat1.at[pl.ds(pl.multiple_of(start + h * BITE, BITE), BITE)],
                    all1.at[x, h * BITE : (h + 1) * BITE],
                    b_send.at[j - 1, h],
                    b_recv.at[j - 1, h],
                    on_x[j],
                )
                for h in (0, 1)
            ]
        )
        b2_copies.append(
            remote(
                hat1.at[pl.ds(pl.multiple_of(start + PART, PART), 3 * PART)],
                all1.at[x, PART:HALF],
                b2_send.at[j - 1],
                b2_recv.at[j - 1],
                on_x[j],
            )
        )
    for c in bites(b_copies):
        c.start()

    total2 = nn(hat1[pl.ds(pl.multiple_of(x * PART, PART), PART)], up_v[1, rank_rows(x)])
    back_v[...] = row_places(inverse_of(local), WIDE)
    back_copy = pltpu.make_async_copy(back_v, back_s, place_sem.at[1])
    back_copy.start()
    loads[2].wait()
    for i in range(B_NEAR):
        near_chunk(i)
    c_copies = spread(hat2, all2.at[gy], c_send, c_recv, on_y)
    for h in (0, 1):
        rows = slice(h * BITE, (h + 1) * BITE)
        part = total2[rows]
        for j in (1, 3, 2):
            s = before(x, j)
            b_copies[j][h].wait_recv()
            part += nn(all1[s, rows], up_v[1, rank_rows(s)])
        hat2[rows] = part.astype(BF16)
        for j in (2, 1, 3):
            c_copies[j][h].start()
    for j in (2, 1, 3):
        b2_copies[j].start()

    total3 = nn(hat2[...], up_v[2, rank_rows(gy)])
    for i in range(B_NEAR, 8):
        near_chunk(i)
    loads[8].wait()
    basis_rows(0)
    basis_rows(1)
    back_copy.wait()
    turn(0, C_TURN)
    d_copies = spread(hat3, all3.at[gx], d_send, d_recv, on_g)
    for h in (0, 1):
        rows = slice(h * BITE, (h + 1) * BITE)
        part = total3[rows]
        for j in (1, 3, 2):
            s = before(gy, j)
            c_copies[j][h].wait_recv()
            part += nn(all2[s, rows], up_v[2, rank_rows(s)])
        hat3[rows] = part.astype(BF16)
        for j in (2, 1, 3):
            d_copies[j][h].start()

    loads[3].wait()
    loads[4].wait()
    far2 = jnp.zeros((PART, RANK), F32)
    for j in (1, 2, 3):
        s = before(gy, j)
        far2 += nt(all2[s], nc_v[1, skip(s, gy)])
    a_copies[2].wait_recv()
    for leaf in range(2):
        far0[leaf] = (
            nt(hat0[1 - leaf], lc_v[leaf, 2 * k])
            + nt(sib0[0], lc_v[leaf, 1 - k])
            + nt(sib0[1], lc_v[leaf, 2 - k])
        )
    turn(C_TURN, D_TURN)
    loads[7].wait()

    e_copies = [None] + [
        [
            remote(
                low2.at[h * BITE : (h + 1) * BITE],
                low2.at[(4 - j) * PART + h * BITE : (4 - j) * PART + (h + 1) * BITE],
                e_send.at[j - 1, h],
                e_recv.at[j - 1, h],
                on_x[j],
            )
            for h in (0, 1)
        ]
        for j in (1, 2, 3)
    ]
    for h in (0, 1):
        rows = slice(h * BITE, (h + 1) * BITE)
        far3 = jnp.zeros((BITE, RANK), F32)
        for j in (1, 3, 2):
            s = before(gx, j)
            d_copies[j][h].wait_recv()
            far3 += nt(all3[s, rows], nc_v[2, skip(s, gx)])
        low2[rows] = (far2[rows] + nt(far3.astype(BF16), dn3_v[...])).astype(BF16)
        for j in (2, 1, 3):
            e_copies[j][h].start()
    total = jnp.zeros((HALF, RANK), F32)
    for j in (1, 2, 3):
        s = before(x, j)
        b2_copies[j].wait_recv()
        total += nt(all1[s], nc_v[0, skip(s, x)])
    far1[...] = total
    turn(C_TURN + D_TURN, GROUPS - C_TURN - D_TURN)
    turned_to_bf16(0, GROUPS)
    loads[6].wait()
    f_copies = []

    def half_rows(core, m, first):
        return core * HALF + lax.rem(x + m, 4) * PART + first

    def low1_block(m, first, count):
        at = m * PART + first
        value = far1[at : at + count] + nt(low2[at : at + count], dn2_v[...])
        rows = pl.ds(pl.multiple_of(half_rows(k, m, first), BITE), count)
        low1[rows] = value.astype(BF16)
        n = len(f_copies)
        f_copies.append(remote(low1.at[rows], low1.at[rows], f_send.at[n], f_recv.at[n], twin))
        f_copies[-1].start()

    blocks = [(0, 0, PART)] + [(m, h * BITE, BITE) for h in (0, 1) for m in (3, 1, 2)]
    for m, first, count in blocks:
        if m:
            e_copies[4 - m][first // BITE].wait_recv()
        low1_block(m, first, count)
    loads[5].wait()

    def leaf_down(rows):
        for leaf in range(2):
            value = far0[leaf, rows] + nt(low1[rows], dn1_v[leaf * RANK : (leaf + 1) * RANK])
            low0[rows, leaf * RANK : (leaf + 1) * RANK] = value.astype(BF16)

    leaf_down(mine)
    for n, (m, first, count) in enumerate(blocks):
        rows = pl.ds(pl.multiple_of(half_rows(1 - k, m, first), BITE), count)
        remote(low1.at[rows], low1.at[rows], f_send.at[n], f_recv.at[n], twin).wait_recv()
    leaf_down(other)

    for c in a_copies + b2_copies[1:] + f_copies:
        c.wait_send()
    for kind in (b_copies, c_copies, d_copies, e_copies):
        for c in bites(kind):
            c.wait_send()


def leaf_kernel(ridge, turned, turned_basis, low0, points, out, out_v, out_sem):
    gain = ridge[0]
    points4 = points.reshape(TILES, LANES, 8, 128)
    turned4 = turned.reshape(TILES, WIDE, 8, 128)
    out4 = out_v.reshape(TILES, LANES, 8, 128)
    copies = []
    for i in range(8):
        block = nt(turned_basis[i * 256 : (i + 1) * 256], low0[...])
        t = i * 32
        for c in range(LANES):
            fixed = turned4[t : t + 32, c] + points4[t : t + 32, c] * gain
            out4[t : t + 32, c] = fixed + block[:, c * 128 : (c + 1) * 128].reshape(32, 8, 128)
        rows = pl.ds(i * (FLAT // 8), FLAT // 8)
        copies.append(pltpu.make_async_copy(out_v.at[rows], out.at[rows], out_sem.at[i]))
        copies[-1].start()
    for c in copies:
        c.wait()


def on_device(
    points,
    order,
    near,
    basis_in,
    basis_out,
    leaf_coupling,
    transfer_up,
    transfer_down,
    node_coupling,
    ridge,
):
    flat_points = points.reshape(TILES, 8, LANES, 128).transpose(0, 2, 1, 3).reshape(FLAT, 128)
    order_rows = order.reshape(ROWS // 128, 128)
    vmem = pl.BlockSpec(memory_space=pltpu.VMEM)
    hbm = pl.BlockSpec(memory_space=pltpu.HBM)
    dma = pltpu.SemaphoreType.DMA
    turned, turned_basis, low0, held_points = pl.pallas_call(
        tree_kernel,
        out_shape=(
            pltpu.VMEM((2 * FLAT, 128), F32),
            pltpu.VMEM((ROWS, COLS), BF16),
            pltpu.VMEM((COLS, 2 * RANK), BF16),
            pltpu.VMEM((FLAT, 128), F32),
        ),
        in_specs=[hbm] * 9,
        out_specs=(vmem, vmem, vmem, vmem),
        scratch_shapes=[
            pltpu.VMEM((2 * FLAT, 128), F32),
            pltpu.VMEM((2, LEAF, RANK), BF16),
            pltpu.VMEM((2, LEAF, LEAF), BF16),
            pltpu.VMEM((2, LEAF, RANK), BF16),
            pltpu.VMEM((2, 3, RANK, RANK), BF16),
            pltpu.VMEM((3, 4 * RANK, RANK), BF16),
            pltpu.VMEM((2 * RANK, RANK), BF16),
            pltpu.VMEM((RANK, RANK), BF16),
            pltpu.VMEM((RANK, RANK), BF16),
            pltpu.VMEM((3, 3, RANK, RANK), BF16),
            pltpu.VMEM((ROWS // 128, 128), jnp.int32),
            pltpu.VMEM((ROWS // 128, 128), jnp.int32),
            pltpu.SMEM((ROWS // 128, 128), jnp.int32),
            pltpu.VMEM((ROWS // 128, 128), jnp.int32),
            pltpu.SMEM((ROWS // 128, 128), jnp.int32),
            pltpu.VMEM((ROWS, COLS), BF16),
            pltpu.VMEM((2, COLS, RANK), BF16),
            pltpu.VMEM((2, COLS, RANK), BF16),
            pltpu.VMEM((2 * HALF, RANK), BF16),
            pltpu.VMEM((4, HALF, RANK), BF16),
            pltpu.VMEM((PART, RANK), BF16),
            pltpu.VMEM((4, PART, RANK), BF16),
            pltpu.VMEM((PART, RANK), BF16),
            pltpu.VMEM((4, PART, RANK), BF16),
            pltpu.VMEM((2, COLS, RANK), F32),
            pltpu.VMEM((HALF, RANK), F32),
            pltpu.VMEM((4 * PART, RANK), BF16),
            pltpu.VMEM((COLS, RANK), BF16),
            dma,
            dma((9,)),
            dma((4,)),
            dma((2,)),
            dma((3,)),
            dma((3,)),
            dma((3, 2)),
            dma((3, 2)),
            dma((3,)),
            dma((3,)),
            dma((3, 2)),
            dma((3, 2)),
            dma((3, 2)),
            dma((3, 2)),
            dma((3, 2)),
            dma((3, 2)),
            dma((7,)),
            dma((7,)),
        ],
        compiler_params=pltpu.CompilerParams(
            collective_id=0, has_side_effects=True, vmem_limit_bytes=40 << 20
        ),
        name="tree",
    )(
        order_rows,
        flat_points,
        near,
        basis_in,
        basis_out,
        leaf_coupling,
        transfer_up,
        transfer_down,
        node_coupling,
    )
    out = pl.pallas_call(
        leaf_kernel,
        out_shape=jax.ShapeDtypeStruct((FLAT, 128), F32),
        in_specs=[pl.BlockSpec(memory_space=pltpu.SMEM)] + [vmem] * 4,
        out_specs=hbm,
        scratch_shapes=[pltpu.VMEM((FLAT, 128), F32), dma((8,))],
        compiler_params=pltpu.CompilerParams(vmem_limit_bytes=12 << 20),
        name="leaves",
    )(ridge, turned, turned_basis, low0, held_points)
    return out.reshape(TILES, LANES, 8, 128).transpose(0, 2, 1, 3).reshape(ROWS, COLS)


def solution(mesh):
    placed = (
        P(("gx", "gy", "gz"), None),
        P(("gx", "gy", "gz")),
        P(("gx", "gy", "gz"), None, None),
        P(("gx", "gy", "gz"), None, None),
        P(("gx", "gy", "gz"), None, None),
        P(("gx", "gy", "gz"), None, None, None),
        P(("gx", "gy", "gz"), None, None, None),
        P(("gx", "gy", "gz"), None, None, None),
        P(("gx", "gy", "gz"), None, None, None, None),
        P(),
    )
    return jax.shard_map(
        on_device,
        mesh=mesh,
        in_specs=placed,
        out_specs=P(("gx", "gy", "gz"), None),
        check_vma=False,
    )
```

```python
import jax
import jax.numpy as jnp
from jax import lax
from jax.experimental import pallas as pl
from jax.experimental.pallas import tpu as pltpu
from jax.sharding import PartitionSpec as P

F32 = jnp.float32
BF16 = jnp.bfloat16
MESH = pl.DeviceIdType.MESH

ROWS = 2048
LEAF = 1024
COLS = 512
RANK = 256
HALF = 256
PART = 64
BITE = PART // 2
TILES = ROWS // 8
LANES = COLS // 128
FLAT = ROWS * LANES
WIDE = 2 * LANES
GROUP = 128
GROUPS = ROWS // GROUP
BATCH = 16
B_NEAR, C_TURN, D_TURN = 5, 4, 6


def nt(a, b):
    return lax.dot_general(a, b, (((1,), (1,)), ((), ())), preferred_element_type=F32)


def nn(a, b):
    return jnp.dot(a, b, preferred_element_type=F32)


def row_places(index, tiles):
    return (index >> 3) * (8 * tiles) + (index & 7)


def inverse_of(local):
    high, low = local >> 7, local & 127
    row_high = lax.broadcasted_iota(jnp.int32, (GROUPS, GROUP), 0)
    row_low = lax.broadcasted_iota(jnp.int32, (GROUP, GROUP), 0)
    lane = lax.broadcasted_iota(jnp.int32, (GROUPS, GROUP), 1).astype(F32)
    total = jnp.zeros((2 * GROUPS, GROUP), F32)
    for b in range(GROUPS):
        hit_high = jnp.where(row_high == high[b : b + 1], 1.0, 0.0)
        hit_low = jnp.where(row_low == low[b : b + 1], 1.0, 0.0).astype(BF16)
        values = jnp.concatenate([hit_high * float(b), hit_high * lane], axis=0).astype(BF16)
        total += nt(values, hit_low)
    return (total[:GROUPS] * float(GROUP) + total[GROUPS:]).astype(jnp.int32) & (ROWS - 1)


def move_rows(places, source, target, tiles, target_tiles, first, count):
    def step(i, _):
        for w in range(GROUP // BATCH):
            rows = []
            for u in range(w * BATCH, (w + 1) * BATCH):
                rows.append(source[pl.ds(places[i, u], tiles, stride=8), :])
            for u in range(w * BATCH, (w + 1) * BATCH):
                to = i * (GROUP * target_tiles) + (u // 8) * (8 * target_tiles) + (u % 8)
                target[pl.ds(to, tiles, stride=8), :] = rows[u - w * BATCH]
        return 0

    lax.fori_loop(first, first + count, step, 0)


def tree_kernel(
    order,
    points,
    near,
    basis_in,
    basis_out,
    leaf_coupling,
    transfer_up,
    transfer_down,
    node_coupling,
    turned,
    turned_basis,
    low0,
    pts_v,
    wide,
    out_basis_v,
    near_v,
    basis_v,
    lc_v,
    up_v,
    dn1_v,
    dn2_v,
    dn3_v,
    nc_v,
    order_v,
    place_v,
    place_s,
    back_v,
    back_s,
    rounded,
    hat0,
    sib0,
    hat1,
    all1,
    hat2,
    all2,
    hat3,
    all3,
    far0,
    far1,
    low2,
    low1,
    order_sem,
    load_sem,
    point_sem,
    place_sem,
    a_send,
    a_recv,
    b_send,
    b_recv,
    b2_send,
    b2_recv,
    c_send,
    c_recv,
    d_send,
    d_recv,
    e_send,
    e_recv,
    f_send,
    f_recv,
):
    gx = lax.axis_index("gx")
    gy = lax.axis_index("gy")
    gz = lax.axis_index("gz")
    x = gz // 2
    k = lax.rem(gz, 2)
    twin = (gx, gy, x * 2 + (1 - k))
    on_x = [None] + [(gx, gy, lax.rem(x + j, 4) * 2 + k) for j in (1, 2, 3)]
    on_y = [None] + [(gx, lax.rem(gy + j, 4), gz) for j in (1, 2, 3)]
    on_g = [None] + [(lax.rem(gx + j, 4), gy, gz) for j in (1, 2, 3)]

    order_copy = pltpu.make_async_copy(order, order_v, order_sem)
    order_copy.start()
    chunk = FLAT // 4
    point_copies = [
        pltpu.make_async_copy(
            points.at[pl.ds(i * chunk, chunk)],
            pts_v.at[pl.ds(i * chunk, chunk)],
            point_sem.at[i],
        )
        for i in range(4)
    ]
    for c in point_copies:
        c.start()
    barrier = pltpu.get_barrier_semaphore()
    for dev in [twin] + on_x[1:] + on_y[1:] + on_g[1:]:
        pl.semaphore_signal(barrier, inc=1, device_id=dev, device_id_type=MESH)

    order_copy.wait()
    local = order_v[...] & (ROWS - 1)
    place_v[...] = row_places(local, LANES)
    place_copy = pltpu.make_async_copy(place_v, place_s, place_sem.at[0])
    place_copy.start()

    def rank_rows(i):
        return pl.ds(pl.multiple_of(i * RANK, RANK), RANK)

    loads = [
        pltpu.make_async_copy(basis_in, basis_v, load_sem.at[0]),
        pltpu.make_async_copy(transfer_up.at[0], up_v, load_sem.at[1]),
        pltpu.make_async_copy(near, near_v, load_sem.at[2]),
        pltpu.make_async_copy(leaf_coupling, lc_v, load_sem.at[3]),
        pltpu.make_async_copy(node_coupling.at[0], nc_v, load_sem.at[4]),
        pltpu.make_async_copy(
            transfer_down.at[0, 0, pl.ds(pl.multiple_of(k * 2 * RANK, 2 * RANK), 2 * RANK)],
            dn1_v,
            load_sem.at[5],
        ),
        pltpu.make_async_copy(transfer_down.at[0, 1, rank_rows(x)], dn2_v, load_sem.at[6]),
        pltpu.make_async_copy(transfer_down.at[0, 2, rank_rows(gy)], dn3_v, load_sem.at[7]),
        pltpu.make_async_copy(basis_out, out_basis_v, load_sem.at[8]),
    ]
    place_copy.wait()
    for c in point_copies:
        c.wait()
    for c in loads:
        c.start()

    move_rows(place_s, pts_v, wide, LANES, WIDE, 0, GROUPS)
    wide4 = wide.reshape(TILES, WIDE, 8, 128)

    def to_bf16(core):
        def step(i, _):
            for tile in range(LANES // 2):
                c = core * (LANES // 2) + tile
                block = wide4[pl.ds(i * 32, 32), c]
                lanes = pl.ds(pl.multiple_of(c * 128, 128), 128)
                rounded[pl.ds(i * 256, 256), lanes] = block.reshape(256, 128).astype(BF16)
            return 0

        lax.fori_loop(0, ROWS // 256, step, 0)

    to_bf16(1 - k)

    loads[0].wait()
    mine = pl.ds(pl.multiple_of(k * HALF, HALF), HALF)
    other = pl.ds(pl.multiple_of((1 - k) * HALF, HALF), HALF)

    def remote(src, dst, send, recv, dev):
        return pltpu.make_async_remote_copy(
            src_ref=src, dst_ref=dst, send_sem=send, recv_sem=recv, device_id=dev, device_id_type=MESH
        )

    def leaf_up(leaf, columns):
        hat0[leaf, columns] = lax.dot_general(
            rounded[leaf * LEAF : (leaf + 1) * LEAF, columns],
            basis_v[leaf],
            (((0,), (0,)), ((), ())),
            preferred_element_type=F32,
        ).astype(BF16)

    a_copies = [
        remote(hat0.at[0, other], sib0.at[0, other], a_send.at[0], a_recv.at[0], twin),
        remote(hat0.at[1, other], sib0.at[1, other], a_send.at[1], a_recv.at[1], twin),
        remote(hat0.at[:, mine], sib0.at[:, mine], a_send.at[2], a_recv.at[2], twin),
    ]
    leaf_up(0, other)
    pl.semaphore_wait(barrier, 10)
    a_copies[0].start()
    leaf_up(1, other)
    a_copies[1].start()
    to_bf16(k)
    leaf_up(0, mine)
    leaf_up(1, mine)
    a_copies[2].start()

    def near_chunk(i):
        leaf, q = i // 4, i % 4
        block = nn(near_v[leaf, q * 256 : (q + 1) * 256], rounded[leaf * LEAF : (leaf + 1) * LEAF])
        t = leaf * 128 + q * 32
        for c in range(LANES):
            wide4[t : t + 32, c] = block[:, c * 128 : (c + 1) * 128].reshape(32, 8, 128)

    def basis_rows(leaf):
        none = jnp.zeros((32, 8, 128), F32)
        for q in range(4):
            t = leaf * 128 + q * 32
            for c in range(2):
                block = out_basis_v[leaf, q * 256 : (q + 1) * 256, c * 128 : (c + 1) * 128]
                wide4[t : t + 32, LANES + leaf * 2 + c] = block.astype(F32).reshape(32, 8, 128)
                wide4[t : t + 32, LANES + (1 - leaf) * 2 + c] = none

    def turn(first, count):
        move_rows(back_s, wide, turned, WIDE, WIDE, first, count)

    turned4 = turned.reshape(TILES, WIDE, 8, 128)

    def turned_to_bf16(first, count):
        def step(i, _):
            for c in range(LANES):
                block = turned4[pl.ds(i * 16, 16), LANES + c]
                turned_basis[pl.ds(i * 128, 128), c * 128 : (c + 1) * 128] = block.reshape(128, 128).astype(BF16)
            return 0

        lax.fori_loop(first, first + count, step, 0)

    def bites(kind):
        return [kind[j][h] for h in (0, 1) for j in (2, 1, 3)]

    def skip(s, own):
        return jnp.where(s > own, s - 1, s)

    def before(own, j):
        return lax.rem(own - j + 4, 4)

    def spread(source, target, send, recv, where):
        return [None] + [
            [
                remote(
                    source.at[h * BITE : (h + 1) * BITE],
                    target.at[h * BITE : (h + 1) * BITE],
                    send.at[j - 1, h],
                    recv.at[j - 1, h],
                    where[j],
                )
                for h in (0, 1)
            ]
            for j in (1, 2, 3)
        ]

    loads[1].wait()
    total1 = nn(hat0[0, mine], up_v[0, rank_rows(2 * k)]) + nn(hat0[1, mine], up_v[0, rank_rows(2 * k + 1)])
    sib = 1 - k
    for leaf in range(2):
        remote(
            hat0.at[leaf, other], sib0.at[leaf, mine], a_send.at[leaf], a_recv.at[leaf], twin
        ).wait_recv()
        total1 += nn(sib0[leaf, mine], up_v[0, rank_rows(2 * sib + leaf)])
    value1 = total1.astype(BF16)
    hat1[0:HALF] = value1
    hat1[HALF : 2 * HALF] = value1
    b_copies, b2_copies = [None], [None]
    for j in (1, 2, 3):
        start = lax.rem(x + j, 4) * PART
        b_copies.append(
            [
                remote(
                    hat1.at[pl.ds(pl.multiple_of(start + h * BITE, BITE), BITE)],
                    all1.at[x, h * BITE : (h + 1) * BITE],
                    b_send.at[j - 1, h],
                    b_recv.at[j - 1, h],
                    on_x[j],
                )
                for h in (0, 1)
            ]
        )
        b2_copies.append(
            remote(
                hat1.at[pl.ds(pl.multiple_of(start + PART, PART), 3 * PART)],
                all1.at[x, PART:HALF],
                b2_send.at[j - 1],
                b2_recv.at[j - 1],
                on_x[j],
            )
        )
    for c in bites(b_copies):
        c.start()

    total2 = nn(hat1[pl.ds(pl.multiple_of(x * PART, PART), PART)], up_v[1, rank_rows(x)])
    back_v[...] = row_places(inverse_of(local), WIDE)
    back_copy = pltpu.make_async_copy(back_v, back_s, place_sem.at[1])
    back_copy.start()
    loads[2].wait()
    for i in range(B_NEAR):
        near_chunk(i)
    c_copies = spread(hat2, all2.at[gy], c_send, c_recv, on_y)
    for h in (0, 1):
        rows = slice(h * BITE, (h + 1) * BITE)
        part = total2[rows]
        for j in (3, 1, 2):
            s = before(x, j)
            b_copies[j][h].wait_recv()
            part += nn(all1[s, rows], up_v[1, rank_rows(s)])
        hat2[rows] = part.astype(BF16)
        for j in (2, 1, 3):
            c_copies[j][h].start()
    for j in (2, 1, 3):
        b2_copies[j].start()

    total3 = nn(hat2[...], up_v[2, rank_rows(gy)])
    for i in range(B_NEAR, 8):
        near_chunk(i)
    loads[8].wait()
    basis_rows(0)
    basis_rows(1)
    back_copy.wait()
    turn(0, C_TURN)
    d_copies = spread(hat3, all3.at[gx], d_send, d_recv, on_g)
    for h in (0, 1):
        rows = slice(h * BITE, (h + 1) * BITE)
        part = total3[rows]
        for j in (3, 1, 2):
            s = before(gy, j)
            c_copies[j][h].wait_recv()
            part += nn(all2[s, rows], up_v[2, rank_rows(s)])
        hat3[rows] = part.astype(BF16)
        for j in (2, 1, 3):
            d_copies[j][h].start()

    loads[3].wait()
    loads[4].wait()
    far2 = jnp.zeros((PART, RANK), F32)
    for j in (1, 2, 3):
        s = before(gy, j)
        far2 += nt(all2[s], nc_v[1, skip(s, gy)])
    a_copies[2].wait_recv()
    for leaf in range(2):
        far0[leaf] = (
            nt(hat0[1 - leaf], lc_v[leaf, 2 * k])
            + nt(sib0[0], lc_v[leaf, 1 - k])
            + nt(sib0[1], lc_v[leaf, 2 - k])
        )
    turn(C_TURN, D_TURN)
    for c in a_copies + bites(b_copies):
        c.wait_send()
    loads[7].wait()

    e_copies = [None] + [
        [
            remote(
                low2.at[h * BITE : (h + 1) * BITE],
                low2.at[(4 - j) * PART + h * BITE : (4 - j) * PART + (h + 1) * BITE],
                e_send.at[j - 1, h],
                e_recv.at[j - 1, h],
                on_x[j],
            )
            for h in (0, 1)
        ]
        for j in (1, 2, 3)
    ]
    for h in (0, 1):
        rows = slice(h * BITE, (h + 1) * BITE)
        far3 = jnp.zeros((BITE, RANK), F32)
        for j in (3, 1, 2):
            s = before(gx, j)
            d_copies[j][h].wait_recv()
            far3 += nt(all3[s, rows], nc_v[2, skip(s, gx)])
        low2[rows] = (far2[rows] + nt(far3.astype(BF16), dn3_v[...])).astype(BF16)
        for j in (2, 1, 3):
            e_copies[j][h].start()
    total = jnp.zeros((HALF, RANK), F32)
    for j in (1, 2, 3):
        s = before(x, j)
        b2_copies[j].wait_recv()
        total += nt(all1[s], nc_v[0, skip(s, x)])
    far1[...] = total
    turn(C_TURN + D_TURN, GROUPS - C_TURN - D_TURN)
    turned_to_bf16(0, GROUPS)
    for c in b2_copies[1:] + bites(c_copies):
        c.wait_send()
    loads[6].wait()
    f_copies = []

    def half_rows(core, m, first):
        return core * HALF + lax.rem(x + m, 4) * PART + first

    def low1_block(m, first, count):
        at = m * PART + first
        value = far1[at : at + count] + nt(low2[at : at + count], dn2_v[...])
        rows = pl.ds(pl.multiple_of(half_rows(k, m, first), BITE), count)
        low1[rows] = value.astype(BF16)
        n = len(f_copies)
        f_copies.append(remote(low1.at[rows], low1.at[rows], f_send.at[n], f_recv.at[n], twin))
        f_copies[-1].start()

    blocks = [(0, 0, PART)] + [(m, h * BITE, BITE) for h in (0, 1) for m in (3, 1, 2)]
    for m, first, count in blocks:
        if m:
            e_copies[4 - m][first // BITE].wait_recv()
        low1_block(m, first, count)
    loads[5].wait()

    def leaf_down(rows):
        for leaf in range(2):
            value = far0[leaf, rows] + nt(low1[rows], dn1_v[leaf * RANK : (leaf + 1) * RANK])
            low0[rows, leaf * RANK : (leaf + 1) * RANK] = value.astype(BF16)

    leaf_down(mine)
    for c in bites(d_copies) + bites(e_copies) + f_copies[:-1]:
        c.wait_send()
    for n, (m, first, count) in enumerate(blocks):
        rows = pl.ds(pl.multiple_of(half_rows(1 - k, m, first), BITE), count)
        remote(low1.at[rows], low1.at[rows], f_send.at[n], f_recv.at[n], twin).wait_recv()
    leaf_down(other)
    f_copies[-1].wait_send()


def leaf_kernel(ridge, turned, turned_basis, low0, points, out, out_v, out_sem):
    gain = ridge[0]
    points4 = points.reshape(TILES, LANES, 8, 128)
    turned4 = turned.reshape(TILES, WIDE, 8, 128)
    out4 = out_v.reshape(TILES, LANES, 8, 128)
    copies = []
    for i in range(8):
        block = nt(turned_basis[i * 256 : (i + 1) * 256], low0[...])
        t = i * 32
        for c in range(LANES):
            fixed = turned4[t : t + 32, c] + points4[t : t + 32, c] * gain
            out4[t : t + 32, c] = fixed + block[:, c * 128 : (c + 1) * 128].reshape(32, 8, 128)
        rows = pl.ds(i * (FLAT // 8), FLAT // 8)
        copies.append(pltpu.make_async_copy(out_v.at[rows], out.at[rows], out_sem.at[i]))
        copies[-1].start()
    for c in copies:
        c.wait()


def on_device(
    points,
    order,
    near,
    basis_in,
    basis_out,
    leaf_coupling,
    transfer_up,
    transfer_down,
    node_coupling,
    ridge,
):
    flat_points = points.reshape(TILES, 8, LANES, 128).transpose(0, 2, 1, 3).reshape(FLAT, 128)
    order_rows = order.reshape(ROWS // 128, 128)
    vmem = pl.BlockSpec(memory_space=pltpu.VMEM)
    hbm = pl.BlockSpec(memory_space=pltpu.HBM)
    dma = pltpu.SemaphoreType.DMA
    turned, turned_basis, low0, held_points = pl.pallas_call(
        tree_kernel,
        out_shape=(
            pltpu.VMEM((2 * FLAT, 128), F32),
            pltpu.VMEM((ROWS, COLS), BF16),
            pltpu.VMEM((COLS, 2 * RANK), BF16),
            pltpu.VMEM((FLAT, 128), F32),
        ),
        in_specs=[hbm] * 9,
        out_specs=(vmem, vmem, vmem, vmem),
        scratch_shapes=[
            pltpu.VMEM((2 * FLAT, 128), F32),
            pltpu.VMEM((2, LEAF, RANK), BF16),
            pltpu.VMEM((2, LEAF, LEAF), BF16),
            pltpu.VMEM((2, LEAF, RANK), BF16),
            pltpu.VMEM((2, 3, RANK, RANK), BF16),
            pltpu.VMEM((3, 4 * RANK, RANK), BF16),
            pltpu.VMEM((2 * RANK, RANK), BF16),
            pltpu.VMEM((RANK, RANK), BF16),
            pltpu.VMEM((RANK, RANK), BF16),
            pltpu.VMEM((3, 3, RANK, RANK), BF16),
            pltpu.VMEM((ROWS // 128, 128), jnp.int32),
            pltpu.VMEM((ROWS // 128, 128), jnp.int32),
            pltpu.SMEM((ROWS // 128, 128), jnp.int32),
            pltpu.VMEM((ROWS // 128, 128), jnp.int32),
            pltpu.SMEM((ROWS // 128, 128), jnp.int32),
            pltpu.VMEM((ROWS, COLS), BF16),
            pltpu.VMEM((2, COLS, RANK), BF16),
            pltpu.VMEM((2, COLS, RANK), BF16),
            pltpu.VMEM((2 * HALF, RANK), BF16),
            pltpu.VMEM((4, HALF, RANK), BF16),
            pltpu.VMEM((PART, RANK), BF16),
            pltpu.VMEM((4, PART, RANK), BF16),
            pltpu.VMEM((PART, RANK), BF16),
            pltpu.VMEM((4, PART, RANK), BF16),
            pltpu.VMEM((2, COLS, RANK), F32),
            pltpu.VMEM((HALF, RANK), F32),
            pltpu.VMEM((4 * PART, RANK), BF16),
            pltpu.VMEM((COLS, RANK), BF16),
            dma,
            dma((9,)),
            dma((4,)),
            dma((2,)),
            dma((3,)),
            dma((3,)),
            dma((3, 2)),
            dma((3, 2)),
            dma((3,)),
            dma((3,)),
            dma((3, 2)),
            dma((3, 2)),
            dma((3, 2)),
            dma((3, 2)),
            dma((3, 2)),
            dma((3, 2)),
            dma((7,)),
            dma((7,)),
        ],
        compiler_params=pltpu.CompilerParams(
            collective_id=0, has_side_effects=True, vmem_limit_bytes=40 << 20
        ),
        name="tree",
    )(
        order_rows,
        flat_points,
        near,
        basis_in,
        basis_out,
        leaf_coupling,
        transfer_up,
        transfer_down,
        node_coupling,
    )
    out = pl.pallas_call(
        leaf_kernel,
        out_shape=jax.ShapeDtypeStruct((FLAT, 128), F32),
        in_specs=[pl.BlockSpec(memory_space=pltpu.SMEM)] + [vmem] * 4,
        out_specs=hbm,
        scratch_shapes=[pltpu.VMEM((FLAT, 128), F32), dma((8,))],
        compiler_params=pltpu.CompilerParams(vmem_limit_bytes=12 << 20),
        name="leaves",
    )(ridge, turned, turned_basis, low0, held_points)
    return out.reshape(TILES, LANES, 8, 128).transpose(0, 2, 1, 3).reshape(ROWS, COLS)


def solution(mesh):
    placed = (
        P(("gx", "gy", "gz"), None),
        P(("gx", "gy", "gz")),
        P(("gx", "gy", "gz"), None, None),
        P(("gx", "gy", "gz"), None, None),
        P(("gx", "gy", "gz"), None, None),
        P(("gx", "gy", "gz"), None, None, None),
        P(("gx", "gy", "gz"), None, None, None),
        P(("gx", "gy", "gz"), None, None, None),
        P(("gx", "gy", "gz"), None, None, None, None),
        P(),
    )
    return jax.shard_map(
        on_device,
        mesh=mesh,
        in_specs=placed,
        out_specs=P(("gx", "gy", "gz"), None),
        check_vma=False,
    )
```

```python
import jax
import jax.numpy as jnp
from jax import lax
from jax.experimental import pallas as pl
from jax.experimental.pallas import tpu as pltpu
from jax.sharding import PartitionSpec as P

F32 = jnp.float32
BF16 = jnp.bfloat16
MESH = pl.DeviceIdType.MESH

ROWS = 2048
LEAF = 1024
COLS = 512
RANK = 256
HALF = 256
PART = 64
BITE = PART // 2
TILES = ROWS // 8
LANES = COLS // 128
FLAT = ROWS * LANES
WIDE = 2 * LANES
GROUP = 128
GROUPS = ROWS // GROUP
BATCH = 16
B_NEAR, C_TURN, D_TURN = 5, 4, 6


def nt(a, b):
    return lax.dot_general(a, b, (((1,), (1,)), ((), ())), preferred_element_type=F32)


def nn(a, b):
    return jnp.dot(a, b, preferred_element_type=F32)


def row_places(index, tiles):
    return (index >> 3) * (8 * tiles) + (index & 7)


def inverse_of(local):
    high, low = local >> 7, local & 127
    row_high = lax.broadcasted_iota(jnp.int32, (GROUPS, GROUP), 0)
    row_low = lax.broadcasted_iota(jnp.int32, (GROUP, GROUP), 0)
    lane = lax.broadcasted_iota(jnp.int32, (GROUPS, GROUP), 1).astype(F32)
    total = jnp.zeros((2 * GROUPS, GROUP), F32)
    for b in range(GROUPS):
        hit_high = jnp.where(row_high == high[b : b + 1], 1.0, 0.0)
        hit_low = jnp.where(row_low == low[b : b + 1], 1.0, 0.0).astype(BF16)
        values = jnp.concatenate([hit_high * float(b), hit_high * lane], axis=0).astype(BF16)
        total += nt(values, hit_low)
    return (total[:GROUPS] * float(GROUP) + total[GROUPS:]).astype(jnp.int32) & (ROWS - 1)


def move_rows(places, source, target, tiles, target_tiles, first, count):
    def step(i, _):
        for w in range(GROUP // BATCH):
            rows = []
            for u in range(w * BATCH, (w + 1) * BATCH):
                rows.append(source[pl.ds(places[i, u], tiles, stride=8), :])
            for u in range(w * BATCH, (w + 1) * BATCH):
                to = i * (GROUP * target_tiles) + (u // 8) * (8 * target_tiles) + (u % 8)
                target[pl.ds(to, tiles, stride=8), :] = rows[u - w * BATCH]
        return 0

    lax.fori_loop(first, first + count, step, 0)


def tree_kernel(
    order,
    points,
    near,
    basis_in,
    basis_out,
    leaf_coupling,
    transfer_up,
    transfer_down,
    node_coupling,
    turned,
    turned_basis,
    low0,
    pts_v,
    wide,
    out_basis_v,
    near_v,
    basis_v,
    lc_v,
    up_v,
    dn1_v,
    dn2_v,
    dn3_v,
    nc_v,
    order_v,
    place_v,
    place_s,
    back_v,
    back_s,
    rounded,
    hat0,
    sib0,
    hat1,
    all1,
    hat2,
    all2,
    hat3,
    all3,
    far0,
    far1,
    low2,
    low1,
    order_sem,
    load_sem,
    point_sem,
    place_sem,
    a_send,
    a_recv,
    b_send,
    b_recv,
    b2_send,
    b2_recv,
    c_send,
    c_recv,
    d_send,
    d_recv,
    e_send,
    e_recv,
    f_send,
    f_recv,
):
    gx = lax.axis_index("gx")
    gy = lax.axis_index("gy")
    gz = lax.axis_index("gz")
    x = gz // 2
    k = lax.rem(gz, 2)
    twin = (gx, gy, x * 2 + (1 - k))
    on_x = [None] + [(gx, gy, lax.rem(x + j, 4) * 2 + k) for j in (1, 2, 3)]
    on_y = [None] + [(gx, lax.rem(gy + j, 4), gz) for j in (1, 2, 3)]
    on_g = [None] + [(lax.rem(gx + j, 4), gy, gz) for j in (1, 2, 3)]

    order_copy = pltpu.make_async_copy(order, order_v, order_sem)
    order_copy.start()
    chunk = FLAT // 4
    point_copies = [
        pltpu.make_async_copy(
            points.at[pl.ds(i * chunk, chunk)],
            pts_v.at[pl.ds(i * chunk, chunk)],
            point_sem.at[i],
        )
        for i in range(4)
    ]
    for c in point_copies:
        c.start()
    barrier = pltpu.get_barrier_semaphore()
    for dev in [twin] + on_x[1:] + on_y[1:] + on_g[1:]:
        pl.semaphore_signal(barrier, inc=1, device_id=dev, device_id_type=MESH)

    order_copy.wait()
    local = order_v[...] & (ROWS - 1)
    place_v[...] = row_places(local, LANES)
    place_copy = pltpu.make_async_copy(place_v, place_s, place_sem.at[0])
    place_copy.start()

    def rank_rows(i):
        return pl.ds(pl.multiple_of(i * RANK, RANK), RANK)

    loads = [
        pltpu.make_async_copy(basis_in, basis_v, load_sem.at[0]),
        pltpu.make_async_copy(transfer_up.at[0], up_v, load_sem.at[1]),
        pltpu.make_async_copy(near, near_v, load_sem.at[2]),
        pltpu.make_async_copy(leaf_coupling, lc_v, load_sem.at[3]),
        pltpu.make_async_copy(node_coupling.at[0], nc_v, load_sem.at[4]),
        pltpu.make_async_copy(
            transfer_down.at[0, 0, pl.ds(pl.multiple_of(k * 2 * RANK, 2 * RANK), 2 * RANK)],
            dn1_v,
            load_sem.at[5],
        ),
        pltpu.make_async_copy(transfer_down.at[0, 1, rank_rows(x)], dn2_v, load_sem.at[6]),
        pltpu.make_async_copy(transfer_down.at[0, 2, rank_rows(gy)], dn3_v, load_sem.at[7]),
        pltpu.make_async_copy(basis_out, out_basis_v, load_sem.at[8]),
    ]
    place_copy.wait()
    for c in point_copies:
        c.wait()
    for c in loads:
        c.start()

    move_rows(place_s, pts_v, wide, LANES, WIDE, 0, GROUPS)
    wide4 = wide.reshape(TILES, WIDE, 8, 128)

    def to_bf16(core):
        def step(i, _):
            for tile in range(LANES // 2):
                c = core * (LANES // 2) + tile
                block = wide4[pl.ds(i * 32, 32), c]
                lanes = pl.ds(pl.multiple_of(c * 128, 128), 128)
                rounded[pl.ds(i * 256, 256), lanes] = block.reshape(256, 128).astype(BF16)
            return 0

        lax.fori_loop(0, ROWS // 256, step, 0)

    to_bf16(1 - k)

    loads[0].wait()
    mine = pl.ds(pl.multiple_of(k * HALF, HALF), HALF)
    other = pl.ds(pl.multiple_of((1 - k) * HALF, HALF), HALF)

    def remote(src, dst, send, recv, dev):
        return pltpu.make_async_remote_copy(
            src_ref=src, dst_ref=dst, send_sem=send, recv_sem=recv, device_id=dev, device_id_type=MESH
        )

    def leaf_up(leaf, columns):
        hat0[leaf, columns] = lax.dot_general(
            rounded[leaf * LEAF : (leaf + 1) * LEAF, columns],
            basis_v[leaf],
            (((0,), (0,)), ((), ())),
            preferred_element_type=F32,
        ).astype(BF16)

    a_copies = [
        remote(hat0.at[0, other], sib0.at[0, other], a_send.at[0], a_recv.at[0], twin),
        remote(hat0.at[1, other], sib0.at[1, other], a_send.at[1], a_recv.at[1], twin),
        remote(hat0.at[:, mine], sib0.at[:, mine], a_send.at[2], a_recv.at[2], twin),
    ]
    leaf_up(0, other)
    pl.semaphore_wait(barrier, 10)
    a_copies[0].start()
    leaf_up(1, other)
    a_copies[1].start()
    to_bf16(k)
    leaf_up(0, mine)
    leaf_up(1, mine)

    def near_chunk(i):
        leaf, q = i // 4, i % 4
        block = nn(near_v[leaf, q * 256 : (q + 1) * 256], rounded[leaf * LEAF : (leaf + 1) * LEAF])
        t = leaf * 128 + q * 32
        for c in range(LANES):
            wide4[t : t + 32, c] = block[:, c * 128 : (c + 1) * 128].reshape(32, 8, 128)

    def basis_rows(leaf):
        none = jnp.zeros((32, 8, 128), F32)
        for q in range(4):
            t = leaf * 128 + q * 32
            for c in range(2):
                block = out_basis_v[leaf, q * 256 : (q + 1) * 256, c * 128 : (c + 1) * 128]
                wide4[t : t + 32, LANES + leaf * 2 + c] = block.astype(F32).reshape(32, 8, 128)
                wide4[t : t + 32, LANES + (1 - leaf) * 2 + c] = none

    def turn(first, count):
        move_rows(back_s, wide, turned, WIDE, WIDE, first, count)

    turned4 = turned.reshape(TILES, WIDE, 8, 128)

    def turned_to_bf16(first, count):
        def step(i, _):
            for c in range(LANES):
                block = turned4[pl.ds(i * 16, 16), LANES + c]
                turned_basis[pl.ds(i * 128, 128), c * 128 : (c + 1) * 128] = block.reshape(128, 128).astype(BF16)
            return 0

        lax.fori_loop(first, first + count, step, 0)

    def bites(kind):
        return [kind[j][h] for h in (0, 1) for j in (2, 1, 3)]

    def skip(s, own):
        return jnp.where(s > own, s - 1, s)

    def before(own, j):
        return lax.rem(own - j + 4, 4)

    def spread(source, target, send, recv, where):
        return [None] + [
            [
                remote(
                    source.at[h * BITE : (h + 1) * BITE],
                    target.at[h * BITE : (h + 1) * BITE],
                    send.at[j - 1, h],
                    recv.at[j - 1, h],
                    where[j],
                )
                for h in (0, 1)
            ]
            for j in (1, 2, 3)
        ]

    loads[1].wait()
    total1 = nn(hat0[0, mine], up_v[0, rank_rows(2 * k)]) + nn(hat0[1, mine], up_v[0, rank_rows(2 * k + 1)])
    sib = 1 - k
    for leaf in range(2):
        remote(
            hat0.at[leaf, other], sib0.at[leaf, mine], a_send.at[leaf], a_recv.at[leaf], twin
        ).wait_recv()
        total1 += nn(sib0[leaf, mine], up_v[0, rank_rows(2 * sib + leaf)])
    value1 = total1.astype(BF16)
    hat1[0:HALF] = value1
    hat1[HALF : 2 * HALF] = value1
    b_copies, b2_copies = [None], [None]
    for j in (1, 2, 3):
        start = lax.rem(x + j, 4) * PART
        b_copies.append(
            [
                remote(
                    hat1.at[pl.ds(pl.multiple_of(start + h * BITE, BITE), BITE)],
                    all1.at[x, h * BITE : (h + 1) * BITE],
                    b_send.at[j - 1, h],
                    b_recv.at[j - 1, h],
                    on_x[j],
                )
                for h in (0, 1)
            ]
        )
        b2_copies.append(
            remote(
                hat1.at[pl.ds(pl.multiple_of(start + PART, PART), 3 * PART)],
                all1.at[x, PART:HALF],
                b2_send.at[j - 1],
                b2_recv.at[j - 1],
                on_x[j],
            )
        )
    for c in bites(b_copies):
        c.start()
    a_copies[2].start()

    total2 = nn(hat1[pl.ds(pl.multiple_of(x * PART, PART), PART)], up_v[1, rank_rows(x)])
    back_v[...] = row_places(inverse_of(local), WIDE)
    back_copy = pltpu.make_async_copy(back_v, back_s, place_sem.at[1])
    back_copy.start()
    loads[2].wait()
    for i in range(B_NEAR):
        near_chunk(i)
    c_copies = spread(hat2, all2.at[gy], c_send, c_recv, on_y)
    for h in (0, 1):
        rows = slice(h * BITE, (h + 1) * BITE)
        part = total2[rows]
        for j in (3, 1, 2):
            s = before(x, j)
            b_copies[j][h].wait_recv()
            part += nn(all1[s, rows], up_v[1, rank_rows(s)])
        hat2[rows] = part.astype(BF16)
        for j in (2, 1, 3):
            c_copies[j][h].start()
    for j in (2, 1, 3):
        b2_copies[j].start()

    total3 = nn(hat2[...], up_v[2, rank_rows(gy)])
    for i in range(B_NEAR, 8):
        near_chunk(i)
    loads[8].wait()
    basis_rows(0)
    basis_rows(1)
    back_copy.wait()
    turn(0, C_TURN)
    d_copies = spread(hat3, all3.at[gx], d_send, d_recv, on_g)
    for h in (0, 1):
        rows = slice(h * BITE, (h + 1) * BITE)
        part = total3[rows]
        for j in (3, 1, 2):
            s = before(gy, j)
            c_copies[j][h].wait_recv()
            part += nn(all2[s, rows], up_v[2, rank_rows(s)])
        hat3[rows] = part.astype(BF16)
        for j in (2, 1, 3):
            d_copies[j][h].start()

    loads[3].wait()
    loads[4].wait()
    far2 = jnp.zeros((PART, RANK), F32)
    for j in (1, 2, 3):
        s = before(gy, j)
        far2 += nt(all2[s], nc_v[1, skip(s, gy)])
    a_copies[2].wait_recv()
    for leaf in range(2):
        far0[leaf] = (
            nt(hat0[1 - leaf], lc_v[leaf, 2 * k])
            + nt(sib0[0], lc_v[leaf, 1 - k])
            + nt(sib0[1], lc_v[leaf, 2 - k])
        )
    turn(C_TURN, D_TURN)
    for c in a_copies + bites(b_copies):
        c.wait_send()
    loads[7].wait()

    e_copies = [None] + [
        [
            remote(
                low2.at[h * BITE : (h + 1) * BITE],
                low2.at[(4 - j) * PART + h * BITE : (4 - j) * PART + (h + 1) * BITE],
                e_send.at[j - 1, h],
                e_recv.at[j - 1, h],
                on_x[j],
            )
            for h in (0, 1)
        ]
        for j in (1, 2, 3)
    ]
    for h in (0, 1):
        rows = slice(h * BITE, (h + 1) * BITE)
        far3 = jnp.zeros((BITE, RANK), F32)
        for j in (3, 1, 2):
            s = before(gx, j)
            d_copies[j][h].wait_recv()
            far3 += nt(all3[s, rows], nc_v[2, skip(s, gx)])
        low2[rows] = (far2[rows] + nt(far3.astype(BF16), dn3_v[...])).astype(BF16)
        for j in (2, 1, 3):
            e_copies[j][h].start()
    total = jnp.zeros((HALF, RANK), F32)
    for j in (1, 2, 3):
        s = before(x, j)
        b2_copies[j].wait_recv()
        total += nt(all1[s], nc_v[0, skip(s, x)])
    far1[...] = total
    turn(C_TURN + D_TURN, GROUPS - C_TURN - D_TURN)
    turned_to_bf16(0, GROUPS)
    for c in b2_copies[1:] + bites(c_copies):
        c.wait_send()
    loads[6].wait()
    f_copies = []

    def half_rows(core, m, first):
        return core * HALF + lax.rem(x + m, 4) * PART + first

    def low1_block(m, first, count):
        at = m * PART + first
        value = far1[at : at + count] + nt(low2[at : at + count], dn2_v[...])
        rows = pl.ds(pl.multiple_of(half_rows(k, m, first), BITE), count)
        low1[rows] = value.astype(BF16)
        n = len(f_copies)
        f_copies.append(remote(low1.at[rows], low1.at[rows], f_send.at[n], f_recv.at[n], twin))
        f_copies[-1].start()

    blocks = [(0, 0, PART)] + [(m, h * BITE, BITE) for h in (0, 1) for m in (1, 3, 2)]
    for m, first, count in blocks:
        if m:
            e_copies[4 - m][first // BITE].wait_recv()
        low1_block(m, first, count)
    loads[5].wait()

    def leaf_down(rows):
        for leaf in range(2):
            value = far0[leaf, rows] + nt(low1[rows], dn1_v[leaf * RANK : (leaf + 1) * RANK])
            low0[rows, leaf * RANK : (leaf + 1) * RANK] = value.astype(BF16)

    leaf_down(mine)
    for c in bites(d_copies) + bites(e_copies) + f_copies[:-1]:
        c.wait_send()
    for n, (m, first, count) in enumerate(blocks):
        rows = pl.ds(pl.multiple_of(half_rows(1 - k, m, first), BITE), count)
        remote(low1.at[rows], low1.at[rows], f_send.at[n], f_recv.at[n], twin).wait_recv()
    leaf_down(other)
    f_copies[-1].wait_send()


def leaf_kernel(ridge, turned, turned_basis, low0, points, out, out_v, out_sem):
    gain = ridge[0]
    points4 = points.reshape(TILES, LANES, 8, 128)
    turned4 = turned.reshape(TILES, WIDE, 8, 128)
    out4 = out_v.reshape(TILES, LANES, 8, 128)
    copies = []
    for i in range(8):
        block = nt(turned_basis[i * 256 : (i + 1) * 256], low0[...])
        t = i * 32
        for c in range(LANES):
            fixed = turned4[t : t + 32, c] + points4[t : t + 32, c] * gain
            out4[t : t + 32, c] = fixed + block[:, c * 128 : (c + 1) * 128].reshape(32, 8, 128)
        rows = pl.ds(i * (FLAT // 8), FLAT // 8)
        copies.append(pltpu.make_async_copy(out_v.at[rows], out.at[rows], out_sem.at[i]))
        copies[-1].start()
    for c in copies:
        c.wait()


def on_device(
    points,
    order,
    near,
    basis_in,
    basis_out,
    leaf_coupling,
    transfer_up,
    transfer_down,
    node_coupling,
    ridge,
):
    flat_points = points.reshape(TILES, 8, LANES, 128).transpose(0, 2, 1, 3).reshape(FLAT, 128)
    order_rows = order.reshape(ROWS // 128, 128)
    vmem = pl.BlockSpec(memory_space=pltpu.VMEM)
    hbm = pl.BlockSpec(memory_space=pltpu.HBM)
    dma = pltpu.SemaphoreType.DMA
    turned, turned_basis, low0, held_points = pl.pallas_call(
        tree_kernel,
        out_shape=(
            pltpu.VMEM((2 * FLAT, 128), F32),
            pltpu.VMEM((ROWS, COLS), BF16),
            pltpu.VMEM((COLS, 2 * RANK), BF16),
            pltpu.VMEM((FLAT, 128), F32),
        ),
        in_specs=[hbm] * 9,
        out_specs=(vmem, vmem, vmem, vmem),
        scratch_shapes=[
            pltpu.VMEM((2 * FLAT, 128), F32),
            pltpu.VMEM((2, LEAF, RANK), BF16),
            pltpu.VMEM((2, LEAF, LEAF), BF16),
            pltpu.VMEM((2, LEAF, RANK), BF16),
            pltpu.VMEM((2, 3, RANK, RANK), BF16),
            pltpu.VMEM((3, 4 * RANK, RANK), BF16),
            pltpu.VMEM((2 * RANK, RANK), BF16),
            pltpu.VMEM((RANK, RANK), BF16),
            pltpu.VMEM((RANK, RANK), BF16),
            pltpu.VMEM((3, 3, RANK, RANK), BF16),
            pltpu.VMEM((ROWS // 128, 128), jnp.int32),
            pltpu.VMEM((ROWS // 128, 128), jnp.int32),
            pltpu.SMEM((ROWS // 128, 128), jnp.int32),
            pltpu.VMEM((ROWS // 128, 128), jnp.int32),
            pltpu.SMEM((ROWS // 128, 128), jnp.int32),
            pltpu.VMEM((ROWS, COLS), BF16),
            pltpu.VMEM((2, COLS, RANK), BF16),
            pltpu.VMEM((2, COLS, RANK), BF16),
            pltpu.VMEM((2 * HALF, RANK), BF16),
            pltpu.VMEM((4, HALF, RANK), BF16),
            pltpu.VMEM((PART, RANK), BF16),
            pltpu.VMEM((4, PART, RANK), BF16),
            pltpu.VMEM((PART, RANK), BF16),
            pltpu.VMEM((4, PART, RANK), BF16),
            pltpu.VMEM((2, COLS, RANK), F32),
            pltpu.VMEM((HALF, RANK), F32),
            pltpu.VMEM((4 * PART, RANK), BF16),
            pltpu.VMEM((COLS, RANK), BF16),
            dma,
            dma((9,)),
            dma((4,)),
            dma((2,)),
            dma((3,)),
            dma((3,)),
            dma((3, 2)),
            dma((3, 2)),
            dma((3,)),
            dma((3,)),
            dma((3, 2)),
            dma((3, 2)),
            dma((3, 2)),
            dma((3, 2)),
            dma((3, 2)),
            dma((3, 2)),
            dma((7,)),
            dma((7,)),
        ],
        compiler_params=pltpu.CompilerParams(
            collective_id=0, has_side_effects=True, vmem_limit_bytes=40 << 20
        ),
        name="tree",
    )(
        order_rows,
        flat_points,
        near,
        basis_in,
        basis_out,
        leaf_coupling,
        transfer_up,
        transfer_down,
        node_coupling,
    )
    out = pl.pallas_call(
        leaf_kernel,
        out_shape=jax.ShapeDtypeStruct((FLAT, 128), F32),
        in_specs=[pl.BlockSpec(memory_space=pltpu.SMEM)] + [vmem] * 4,
        out_specs=hbm,
        scratch_shapes=[pltpu.VMEM((FLAT, 128), F32), dma((8,))],
        compiler_params=pltpu.CompilerParams(vmem_limit_bytes=12 << 20),
        name="leaves",
    )(ridge, turned, turned_basis, low0, held_points)
    return out.reshape(TILES, LANES, 8, 128).transpose(0, 2, 1, 3).reshape(ROWS, COLS)


def solution(mesh):
    placed = (
        P(("gx", "gy", "gz"), None),
        P(("gx", "gy", "gz")),
        P(("gx", "gy", "gz"), None, None),
        P(("gx", "gy", "gz"), None, None),
        P(("gx", "gy", "gz"), None, None),
        P(("gx", "gy", "gz"), None, None, None),
        P(("gx", "gy", "gz"), None, None, None),
        P(("gx", "gy", "gz"), None, None, None),
        P(("gx", "gy", "gz"), None, None, None, None),
        P(),
    )
    return jax.shard_map(
        on_device,
        mesh=mesh,
        in_specs=placed,
        out_specs=P(("gx", "gy", "gz"), None),
        check_vma=False,
    )
```
